32 devices in a mesh: dp: 8 (over z, y), mp: 4 (over x, core).
Axes of the slice: x: 2, y: 2, z: 4, core: 2. Of those that a mesh axis runs over, the one named last changes fastest.
Arguments:
- tokens_in: bfloat16 [256, 196, 768], P('dp', None, 'mp'), may hold values from -60 to 60
- cotangent: bfloat16 [256, 196, 768], P(('dp', 'mp')), may hold values from -6 to 6
- ln1_gain: float32 [768], replicated, may hold values from 0.1 to 1.9
- ln1_bias: float32 [768], replicated, may hold values from -3 to 3
- tok_w1: bfloat16 [196, 384], replicated, may hold values from -0.4375 to 0.4375
- tok_b1: float32 [384], replicated, may hold values from -3 to 3
- tok_w2: bfloat16 [384, 196], replicated, may hold values from -0.3125 to 0.3125
- tok_b2: float32 [196], replicated, may hold values from -3 to 3
- second_norm_gain: float32 [768], replicated, may hold values from 0.1 to 1.9
- second_norm_bias: float32 [768], replicated, may hold values from -3 to 3
- chan_w1: bfloat16 [768, 3072], replicated, may hold values from -0.21875 to 0.21875
- chan_b1: float32 [3072], replicated, may hold values from -3 to 3
- chan_w2: bfloat16 [3072, 768], replicated, may hold values from -0.109375 to 0.109375
- chan_b2: float32 [768], replicated, may hold values from -3 to 3
Outputs:
- output: bfloat16 [256, 196, 768], P(('dp', 'mp'))
- tokens_grad: bfloat16 [256, 196, 768], P('dp', None, 'mp')
- ln1_gain_grad: float32 [768], replicated
- ln1_bias_grad: float32 [768], replicated
- tok_w1_grad: float32 [196, 384], replicated
- tok_b1_grad: float32 [384], replicated
- tok_w2_grad: float32 [384, 196], replicated
- tok_b2_grad: float32 [196], replicated
- ln2_gain_grad: float32 [768], replicated
- ln2_bias_grad: float32 [768], replicated
- chan_w1_grad: float32 [768, 3072], replicated
- chan_b1_grad: float32 [3072], replicated
- chan_w2_grad: float32 [3072, 768], replicated
- chan_b2_grad: float32 [768], replicated
The draws below stay inside these ranges and needn't reach their ends.
All inputs are finite; a program needn't handle non-finite values.
Results may differ from the reference program's by a relative error of at most 0.0076.
Values may be sent and summed in bfloat16 or wider, within the bound.
A program may use at most 256 MiB of HBM per device.

```python
import jax
import jax.numpy as jnp
from jax import lax

D = 768
DS = 384
DC = 3072
S = 196
IMG_MB = 8
IMAGES = 256


def draw_tokens_in(key, part):
    key = jax.random.fold_in(key, 11)
    key_base, key_chan, key_rows = jax.random.split(key, 3)
    channel = 3.0 ** (jnp.arange(D, dtype=jnp.float32) / (D - 1)) * jnp.exp(jax.random.uniform(key_chan, (D,), minval=-0.35, maxval=0.35))
    rows = jnp.exp(jax.random.uniform(key_rows, (IMAGES, S, 1), minval=0.0, maxval=2.3026)) / 3.0
    base = jax.random.truncated_normal(key_base, -4.0, 4.0, (IMAGES, S, D))
    return (base * rows * channel).astype(jnp.bfloat16)


def levels(rng, extent, cuts, least, top_value):
    level, own = 1.0, jax.random.fold_in(rng, 6)
    for position, parts in cuts:
        draws = jnp.exp(jax.random.uniform(jax.random.fold_in(own, position), (parts,), jnp.float32, least / len(cuts), top_value / len(cuts)))
        level = level * jnp.repeat(draws, extent[position] // parts).reshape([-1 if axis == position else 1 for axis in range(len(extent))])
    return level


def centred(stream_key, dims, spread, reach, pieces=(), kind=jnp.bfloat16):
    factor_of = levels(stream_key, dims, pieces, -0.22, 0.18) if pieces else 1.0
    values = jax.random.normal(stream_key, dims, jnp.float32) * spread * factor_of
    return jnp.minimum(jnp.maximum(values, -reach), reach).astype(kind)


def setup_inputs(seed: int = 0) -> dict:
    key_list = jax.random.split(jax.random.key(seed), 15)
    tokens_in = draw_tokens_in(jax.random.fold_in(key_list[14], 71), 0)
    cotangent = centred(key_list[1], (IMAGES, S, D), 1.0, 6.0, ((0, 32),))
    ln1_gain = jnp.clip(1.0 + 0.18 * jax.random.normal(key_list[2], (D,), jnp.float32), 0.1, 1.9)
    ln1_bias = centred(key_list[3], (D,), 0.5, 3.0, (), jnp.float32)
    tok_w1 = centred(key_list[4], (S, DS), S ** -0.5, 0.4375)
    tok_b1 = centred(key_list[5], (DS,), 0.5, 3.0, (), jnp.float32)
    tok_w2 = centred(key_list[6], (DS, S), DS ** -0.5, 0.3125)
    tok_b2 = centred(key_list[7], (S,), 0.5, 3.0, (), jnp.float32)
    second_norm_gain = jnp.clip(1.0 + 0.18 * jax.random.normal(key_list[8], (D,), jnp.float32), 0.1, 1.9)
    second_norm_bias = centred(key_list[9], (D,), 0.5, 3.0, (), jnp.float32)
    chan_w1 = centred(key_list[10], (D, DC), D ** -0.5, 0.21875)
    chan_b1 = centred(key_list[11], (DC,), 0.5, 3.0, (), jnp.float32)
    chan_w2 = centred(key_list[12], (DC, D), DC ** -0.5, 0.109375)
    chan_b2 = centred(key_list[13], (D,), 0.5, 3.0, (), jnp.float32)
    return dict(tokens_in=tokens_in, cotangent=cotangent, ln1_gain=ln1_gain, ln1_bias=ln1_bias, tok_w1=tok_w1, tok_b1=tok_b1, tok_w2=tok_w2, tok_b2=tok_b2, second_norm_gain=second_norm_gain, second_norm_bias=second_norm_bias, chan_w1=chan_w1, chan_b1=chan_b1, chan_w2=chan_w2, chan_b2=chan_b2)


EPS = 1e-06
HIGH = lax.Precision.HIGHEST

@jax.custom_vjp
def low(v):
    return lax.optimization_barrier(v.astype(jnp.bfloat16)).astype(jnp.float32)

@jax.custom_vjp
def low_back(v):
    return v

def low_keep(v):
    return (low(v), None)

def low_pass(saved_residuals, grad):
    return (grad,)

def back_keep(v):
    return (v, None)

def back_low(saved_residuals, grad):
    return (low(grad),)
low.defvjp(low_keep, low_pass)
low_back.defvjp(back_keep, back_low)

def normalize(value_entries, gain_vector, bias_vector):
    mean_value = lax.optimization_barrier(jnp.mean(value_entries, axis=-1, keepdims=True))
    var = lax.optimization_barrier(jnp.mean(value_entries * value_entries, axis=-1, keepdims=True)) - mean_value * mean_value
    return (value_entries - mean_value) * lax.rsqrt(var + EPS) * gain_vector + bias_vector

def layer(block, params):
    g1, c1, tw1, tb1, tw2, tb2, g2, c2, cw1, cb1, cw2, cb2 = params
    normed1 = low(normalize(block, g1, c1))
    token_preactivation = low_back(jnp.einsum('bsc,sh->bhc', normed1, tw1, precision=HIGH) + tb1[None, :, None])
    token_activation = low(jax.nn.gelu(token_preactivation, approximate=False))
    mid = low_back(low(block + jnp.einsum('bhc,hs->bsc', token_activation, tw2, precision=HIGH) + tb2[None, :, None]))
    normed2 = low(normalize(mid, g2, c2))
    pre_chan = low_back(jnp.einsum('bsc,ch->bsh', normed2, cw1, precision=HIGH) + cb1)
    act_chan = low(jax.nn.gelu(pre_chan, approximate=False))
    return mid + jnp.einsum('bsh,hc->bsc', act_chan, cw2, precision=HIGH) + cb2

def reference(tokens_in, cotangent, ln1_gain, ln1_bias, tok_w1, tok_b1, tok_w2, tok_b2, second_norm_gain, second_norm_bias, chan_w1, chan_b1, chan_w2, chan_b2):
    params = tuple((a.astype(jnp.float32) for a in (ln1_gain, ln1_bias, tok_w1, tok_b1, tok_w2, tok_b2, second_norm_gain, second_norm_bias, chan_w1, chan_b1, chan_w2, chan_b2)))
    blocks = tokens_in.astype(jnp.float32).reshape(IMAGES // IMG_MB, IMG_MB, S, D)
    upstream = cotangent.astype(jnp.float32).reshape(IMAGES // IMG_MB, IMG_MB, S, D)

    def step(total, pair):
        block, upstream_block = pair
        result, pullback = jax.vjp(layer, block, params)
        grad_in, grad_params = pullback(upstream_block)
        total = tuple((t + g for t, g in zip(total, grad_params)))
        return (total, (result, grad_in))
    start = tuple((jnp.zeros_like(p) for p in params))
    total, (results, grads_in) = lax.scan(step, start, (blocks, upstream))
    output = results.reshape(IMAGES, S, D).astype(jnp.bfloat16)
    tokens_grad = grads_in.reshape(IMAGES, S, D).astype(jnp.bfloat16)
    return (output, tokens_grad) + total
```

```python
import functools

import jax
import jax.numpy as jnp
from jax import lax
from jax.experimental import pallas as pl
from jax.experimental.pallas import tpu as pltpu
from jax.sharding import PartitionSpec as P

BF = jnp.bfloat16
F32 = jnp.float32
EPS = 1e-06
MESH = pl.DeviceIdType.MESH
NT = (((1,), (1,)), ((), ()))

BLOCK = 512
POINTS = 3
SLOTS = 3
SPACE = 256
LAGS = (0, 1, 4, 6, 7, 8, 9, 10, 12, 15, 16)


def dot(a, b):
    return jnp.dot(a, b, preferred_element_type=F32)


def dot_nt(a, b):
    return lax.dot_general(a, b, NT, preferred_element_type=F32)


def gelu_both(v):
    cdf = 0.5 + 0.5 * lax.erf(v * 0.7071067811865476)
    return v * cdf, cdf + v * (jnp.exp(-0.5 * v * v) * 0.3989422804014327)


def standardize(v, axis):
    width = v.shape[axis]
    mean = jnp.sum(v, axis=axis, keepdims=True) / width
    square = jnp.sum(v * v, axis=axis, keepdims=True) / width
    rstd = lax.rsqrt(square - mean * mean + EPS)
    return (v - mean) * rstd, rstd


def bits_of(n):
    return n.bit_length() - 1


def reduce_plan(n_mp, n_dp, width):
    dp = [("dp", b) for b in range(bits_of(n_dp))]
    mp = [("mp", b) for b in range(1, bits_of(n_mp))]
    if len(dp) == 3 and len(mp) == 1:
        cut = width * 2 // 3
        raw = [(0, cut, [dp[0], mp[0], dp[1], dp[2]]), (cut, width - cut, [dp[1], dp[2], dp[0], mp[0]])]
    else:
        raw = [(0, width, dp + mp)]
    streams = []
    for base, rows, keys in raw:
        stages, have = [], rows
        for key in keys:
            halved = have % 32 == 0
            have = have // 2 if halved else have
            stages.append((key, have, halved))
        streams.append((base, rows, stages))
    return streams


def dp_groups(n_dp):
    groups, stride = [], 1
    while stride < n_dp:
        size = min(8, n_dp // stride)
        groups.append((stride, size))
        stride *= size
    return groups


def layer_kernel(
    n_mp,
    n_dp,
    streams,
    groups,
    tokens,
    cot,
    w1,
    w2,
    g1,
    c1,
    tw1,
    tb1,
    tw2,
    tb2,
    g2,
    c2,
    b1,
    b2,
    out_o,
    dtok_o,
    gw_o,
    smt_o,
    smv_o,
    x_in,
    g_in,
    mid_p,
    g_f,
    g_t,
    n2_f,
    n2_t,
    act_t,
    slope_t,
    out_a,
    dn_a,
    act_s,
    dp_s,
    w1_s,
    w2_s,
    part,
    r0,
    rest,
    n1_s,
    dm_s,
    dm_t,
    tw1p,
    tw1t,
    tw2p,
    tw2t,
    rows_s,
    b1_s,
    cols_s,
    cb1_a,
    va,
    ln1_a,
    tg_a,
    t_b,
    t_r1,
    t_s1,
    t_r2,
    t_s2,
    t_g,
    v_b,
    v_r1,
    v_s1,
    v_r2,
    in_s,
    in_r,
    in_l,
    g_l,
    w_l,
    o_l,
    out_s,
    out_r,
    out_l,
    rs_s,
    rs_r,
    ag_s,
    ag_r,
    own_l,
    sm_s,
    sm_r,
    sm_l,
):
    images, width, patches = x_in.shape
    local = tokens.shape[1]
    hidden = tw1.shape[1]
    blocks = w1.shape[1] // BLOCK
    total = images * patches
    half = total // 2
    mp_me = lax.axis_index("mp")
    dp_me = lax.axis_index("dp")

    def bit_of(key):
        axis, b = key
        me = mp_me if axis == "mp" else dp_me
        return (me // (1 << b)) % 2

    def partner(key):
        axis, b = key
        me = mp_me if axis == "mp" else dp_me
        return {axis: me + (1 << b) * (1 - 2 * bit_of(key))}

    def member(group):
        stride, size = group
        return (dp_me // stride) % size

    def peer(group, k):
        stride, size = group
        mine = member(group)
        other = lax.rem(mine + k, size)
        return other, {"dp": dp_me + (other - mine) * stride}

    def mp_peer(k):
        other = lax.rem(mp_me + k, n_mp)
        return other, {"mp": other}

    def remote(src, dst, send, recv, to):
        return pltpu.make_async_remote_copy(
            src_ref=src, dst_ref=dst, send_sem=send, recv_sem=recv, device_id=to, device_id_type=MESH
        )

    barrier = pltpu.get_barrier_semaphore()
    count = 0
    for k in range(1, n_mp):
        pl.semaphore_signal(barrier, inc=1, device_id=mp_peer(k)[1], device_id_type=MESH)
        count += 1
    for group in groups:
        for k in range(1, group[1]):
            pl.semaphore_signal(barrier, inc=1, device_id=peer(group, k)[1], device_id_type=MESH)
            count += 1

    def channels(member):
        return pl.ds(pl.multiple_of(member * local, 16), local)

    def own_tokens(b):
        return pltpu.make_async_copy(tokens.at[mp_me * images + b], x_in.at[b, channels(mp_me)], in_l.at[b])

    own_cot = pltpu.make_async_copy(cot, n2_f, g_l.at[0])

    def weights(j):
        slot = lax.rem(j, 2)
        cols = pl.ds(pl.multiple_of(j * BLOCK, BLOCK), BLOCK)
        return (
            pltpu.make_async_copy(w1.at[:, cols], w1_s.at[slot], w_l.at[0, slot]),
            pltpu.make_async_copy(w2.at[cols], w2_s.at[slot], w_l.at[1, slot]),
        )

    def load_own(b, _):
        own_tokens(b).start()
        return 0

    own_cot.start()
    lax.fori_loop(0, images, load_own, 0)
    for copy in weights(0):
        copy.start()

    pl.semaphore_wait(barrier, count)

    def token_copy(k, b):
        other, to = mp_peer(k)
        return remote(
            tokens.at[other * images + b], x_in.at[b, channels(mp_me)], in_s.at[k - 1, b], in_r.at[mp_me, b], to
        )

    def send_tokens(b, _):
        for k in range(1, n_mp):
            token_copy(k, b).start()
        return 0

    lax.fori_loop(0, images, send_tokens, 0)

    for row, ref in ((0, g1), (1, c1), (2, g2), (3, c2), (4, b2)):
        rows_s[row : row + 1, :] = ref[...].reshape(1, width)
    for j in range(blocks):
        b1_s[j, 0:1, :] = b1[j * BLOCK : (j + 1) * BLOCK].reshape(1, BLOCK)
    rows_s[5:6, 0:hidden] = tb1[...].reshape(1, hidden)
    rows_s[6:7, 0:patches] = tb2[...].reshape(1, patches)
    cols_s[0] = jnp.broadcast_to(rows_s[0:1, :], (128, width)).T
    cols_s[1] = jnp.broadcast_to(rows_s[1:2, :], (128, width)).T
    tw1p[...] = jnp.zeros_like(tw1p)
    tw1p[0:patches, :] = tw1[...]
    tw1t[...] = tw1p[...].T
    tw2t[...] = jnp.zeros_like(tw2t)
    tw2t[0:patches, :] = tw2[...]
    tw2p[...] = tw2t[...].T
    n1_s[...] = jnp.zeros_like(n1_s)
    dm_s[...] = jnp.zeros_like(dm_s)
    va[...] = jnp.zeros_like(va)
    ln1_a[...] = jnp.zeros_like(ln1_a)
    dm_t[...] = jnp.zeros_like(dm_t)
    tg_a[...] = jnp.zeros_like(tg_a)
    cb1_a[...] = jnp.zeros_like(cb1_a)
    v_b[...] = jnp.zeros_like(v_b)

    own_cot.wait()
    for c in range(0, width, 128):
        cols = slice(c, c + 128)
        wide = n2_f[:, cols].astype(F32)
        va[4:5, cols] = jnp.sum(wide, axis=0, keepdims=True)
        lane = c // 128
        dn_a[lane] = wide
        for b in range(images):
            g_f[b * patches : (b + 1) * patches, cols] = dn_a[lane, pl.ds(b, patches, stride=images), :].astype(BF)
    dn_a[...] = jnp.zeros_like(dn_a)

    def transpose_rows(src, dst):
        for lo in range(0, total, 128):
            hi = min(lo + 128, total)
            dst[:, lo:hi] = src[lo:hi, :].T

    transpose_rows(g_f, g_t)

    def token_forward(b, _):
        for k in range(1, n_mp):
            other, to = mp_peer(k)
            remote(
                tokens.at[mp_me * images + b],
                x_in.at[b, channels(other)],
                in_s.at[k - 1, b],
                in_r.at[other, b],
                to,
            ).wait_recv()
        own_tokens(b).wait()
        x = x_in[b].astype(F32)
        xhat, _ = standardize(x, 0)
        n1_s[:, 0:patches] = (xhat * cols_s[0, :, 0:1] + cols_s[1, :, 0:1]).astype(BF)
        act, slope = gelu_both(dot(n1_s[...], tw1p[...]) + rows_s[5:6, 0:hidden])
        act = act.astype(BF)
        act_t[b] = act
        slope_t[b] = slope.astype(BF)
        mixed = dot(act, tw2p[...])[:, 0:patches] + rows_s[6:7, 0:patches]
        dm_t[:, 0:patches] = (x + mixed).astype(BF)
        mid_p[b] = dm_t[...].T[0:patches, :]
        return 0

    lax.fori_loop(0, images, token_forward, 0)

    for b in range(images):
        mid = mid_p[b].astype(F32)
        xhat, _ = standardize(mid, 1)
        rows = slice(b * patches, (b + 1) * patches)
        n2_f[rows, :] = (xhat * rows_s[2:3, :] + rows_s[3:4, :]).astype(BF)
        out_a[rows, :] = mid + rows_s[4:5, :]
    transpose_rows(n2_f, n2_t)

    core = ("mp", 0)
    core_bit = bit_of(core)

    ids = {}
    for s, (_, _, stages) in enumerate(streams):
        for t in range(len(stages)):
            ids[s, t] = 1 + len(ids)
    held = []
    for base, rows, stages in streams:
        line, off = [(base, rows)], base
        for key, have, halved in stages:
            off = off + bit_of(key) * have if halved else off
            line.append((off, have))
        held.append(line)

    def region(s, t, j):
        off, rows = held[s][t]
        if not isinstance(off, int):
            off = pl.multiple_of(off, 16)
        return gw_o.at[core_bit, pl.ds(off, rows), pl.ds(pl.multiple_of(j * BLOCK, BLOCK), BLOCK)]

    def sums(s, t, j):
        ref = rest[ids[s, t] - 1]
        return ref.at[lax.rem(j, ref.shape[0])]

    def source(s, t, j):
        base, _, _ = streams[s]
        return (r0.at[lax.rem(j, SLOTS)], base) if t == 0 else (sums(s, t - 1, j), 0)

    def core_copy(j):
        return remote(part.at[1 - core_bit], r0.at[lax.rem(j, SLOTS)], rs_s.at[0, j], rs_r.at[0, j], partner(core))

    def stage_copy(s, t, j):
        key, rows, halved = streams[s][2][t]
        ref, low = source(s, t, j)
        low = low + (1 - bit_of(key)) * rows if halved else low
        if not isinstance(low, int):
            low = pl.multiple_of(low, 16)
        i = ids[s, t]
        return remote(ref.at[pl.ds(low, rows)], sums(s, t, j), rs_s.at[i, j], rs_r.at[i, j], partner(key))

    def add_rows(dst, src, low, rows):
        chunk = next(c for c in (64, 48, 32, 16) if rows % c == 0)

        def step(i, _):
            here = pl.ds(pl.multiple_of(i * chunk, 16), chunk)
            there = pl.ds(pl.multiple_of(low + i * chunk, 16), chunk)
            dst[here, :] = (dst[here, :].astype(F32) + src[there, :].astype(F32)).astype(BF)
            return 0

        lax.fori_loop(0, rows // chunk, step, 0)

    def finish_core(j):
        core_copy(j).wait()
        add_rows(r0.at[lax.rem(j, SLOTS)], part.at[core_bit], 0, width)

    def finish_stage(s, t, j):
        stage_copy(s, t, j).wait()
        key, rows, halved = streams[s][2][t]
        ref, low = source(s, t, j)
        add_rows(sums(s, t, j), ref, low + bit_of(key) * rows if halved else low, rows)

    gathers = [[t for t in reversed(range(len(stages))) if stages[t][2]] for _, _, stages in streams]

    def own_copy(s, j):
        last = len(streams[s][2])
        return pltpu.make_async_copy(sums(s, last - 1, j), region(s, last, j), own_l.at[s, j])

    def gather_copy(s, a, j):
        t = gathers[s][a]
        key = streams[s][2][t][0]
        here = region(s, t + 1, j)
        src = sums(s, len(streams[s][2]) - 1, j) if a == 0 else here
        i = ids[s, t]
        return remote(src, here, ag_s.at[i, j], ag_r.at[i, j], partner(key))

    def gather_core(j):
        here = gw_o.at[core_bit, :, pl.ds(pl.multiple_of(j * BLOCK, BLOCK), BLOCK)]
        return remote(here, here, ag_s.at[0, j], ag_r.at[0, j], partner(core))

    n_rs = len(streams[0][2])
    n_ag = len(gathers[0])
    every = range(len(streams))

    def advance(step, j):
        if step == 0:
            core_copy(j).start()
        elif step <= n_rs:
            if step == 1:
                finish_core(j)
            else:
                for s in every:
                    finish_stage(s, step - 2, j)
            for s in every:
                stage_copy(s, step - 1, j).start()
        elif step == n_rs + 1:
            for s in every:
                finish_stage(s, n_rs - 1, j)
                own_copy(s, j).start()
                gather_copy(s, 0, j).start()
        elif step <= n_rs + n_ag + 1:
            a = step - n_rs - 1
            for s in every:
                gather_copy(s, a - 1, j).wait()
                if a == 1:
                    own_copy(s, j).wait()
            if a < n_ag:
                for s in every:
                    gather_copy(s, a, j).start()
            else:
                gather_core(j).start()
        else:
            gather_core(j).wait()

    n_steps = n_rs + n_ag + 3
    lags = list(LAGS[:n_steps])
    while len(lags) < n_steps:
        lags.append(lags[-1] + 1)

    def points(i, p):
        for step in reversed(range(n_steps)):
            lag = lags[step] + POINTS - 1
            if lag % POINTS == p:
                j = i - lag // POINTS

                @pl.when((j >= 0) & (j < blocks))
                def _():
                    advance(step, j)

    def unit(h, j):
        slot = lax.rem(j, 2)
        rows = slice(h * half, (h + 1) * half)
        for lo in range(0, BLOCK, 256):
            cols = slice(lo, lo + 256)
            act, slope = gelu_both(dot(n2_f[rows, :], w1_s[slot, :, cols]) + b1_s[j, 0:1, cols])
            act_s[rows, cols] = act.astype(BF)
            dp = dot_nt(g_f[rows, :], w2_s[slot, cols, :]) * slope
            cb1_a[j, 0:1, cols] += jnp.sum(dp, axis=0, keepdims=True)
            dp_s[rows, cols] = dp.astype(BF)
        out_a[rows, :] += dot(act_s[rows, :], w2_s[slot])
        dn = dot_nt(dp_s[rows, :], w1_s[slot])
        for lane in range(width // 128):
            dn_a[lane, rows, :] += dn[:, lane * 128 : (lane + 1) * 128]

    def block_step(j, _):
        for copy in weights(j):
            copy.wait()

        @pl.when(j + 1 < blocks)
        def _():
            for copy in weights(j + 1):
                copy.start()

        unit(0, j)
        points(j, 0)
        unit(1, j)
        points(j, 1)
        part[0] = dot(n2_t[...], dp_s[...]).astype(BF)
        part[1] = dot(g_t[...], act_s[...]).astype(BF)
        points(j, 2)
        return 0

    lax.fori_loop(0, blocks, block_step, 0)

    def grad_copy(k, b):
        other, to = mp_peer(k)
        return remote(
            x_in.at[b, channels(other)], dtok_o.at[mp_me * images + b], out_s.at[k - 1, b], out_r.at[mp_me, b], to
        )

    def own_grad(b):
        return pltpu.make_async_copy(x_in.at[b, channels(mp_me)], dtok_o.at[mp_me * images + b], out_l.at[b])

    def token_backward(t, odd):
        b = 2 * t + odd
        rows = slice(odd * patches, (odd + 1) * patches)
        xhat2, rstd2 = standardize(mid_p[b].astype(F32), 1)
        both = dn_a.at[:, pl.ds(pl.multiple_of(2 * patches * t, 8), 2 * patches)]
        dn2 = jnp.concatenate([both[lane, rows, :] for lane in range(width // 128)], axis=1)
        for q in range(4):

            @pl.when(b % 4 == q)
            def _():
                quad = g_f.at[pl.ds(pl.multiple_of(4 * patches * (b // 4), 16), 4 * patches)]
                g_in[...] = quad[q * patches : (q + 1) * patches, :]

        va[2:3, :] += jnp.sum(dn2 * xhat2, axis=0, keepdims=True)
        va[3:4, :] += jnp.sum(dn2, axis=0, keepdims=True)
        dxh = dn2 * rows_s[2:3, :]
        first = jnp.sum(dxh, axis=-1, keepdims=True) / width
        second = jnp.sum(dxh * xhat2, axis=-1, keepdims=True) / width
        dm_s[0:patches, :] = (g_in[...].astype(F32) + rstd2 * (dxh - first - xhat2 * second)).astype(BF)
        dm_t[...] = dm_s[...].T
        d_mid = dm_t[:, 0:patches].astype(F32)
        va[6:7, 0:patches] += jnp.sum(d_mid, axis=0, keepdims=True)
        d_pre = dot(dm_t[...], tw2t[...]) * slope_t[b].astype(F32)
        va[5:6, 0:hidden] += jnp.sum(d_pre, axis=0, keepdims=True)
        d_pre = d_pre.astype(BF)
        tg_a[SPACE:, :] += dot(dm_s[...], act_t[b])
        xhat1, rstd1 = standardize(x_in[b].astype(F32), 0)
        n1_s[:, 0:patches] = (xhat1 * cols_s[0, :, 0:1] + cols_s[1, :, 0:1]).astype(BF)
        tg_a[0:SPACE, :] += dot(n1_s[...].T, d_pre)
        dn1 = dot(d_pre, tw1t[...])[:, 0:patches]
        ln1_a[:, 0:1] += jnp.sum(dn1 * xhat1, axis=1, keepdims=True)
        ln1_a[:, 1:2] += jnp.sum(dn1, axis=1, keepdims=True)
        dxh = dn1 * cols_s[0, :, 0:1]
        first = jnp.sum(dxh, axis=0, keepdims=True) / width
        second = jnp.sum(dxh * xhat1, axis=0, keepdims=True) / width
        x_in[b] = (d_mid + rstd1 * (dxh - first - xhat1 * second)).astype(BF)
        for k in range(1, n_mp):
            grad_copy(k, b).start()
        own_grad(b).start()

    def wait_tokens(b, _):
        for k in range(1, n_mp):
            token_copy(k, b).wait_send()
        return 0

    lax.fori_loop(0, images, wait_tokens, 0)

    pairs = images // 2
    last_point = POINTS * (blocks - 1) + POINTS - 1 + lags[-1]

    def drain(t, _):
        @pl.when(t < pairs)
        def _():
            token_backward(t, 0)

        points(blocks + t, 0)

        @pl.when(t < pairs)
        def _():
            token_backward(t, 1)

        points(blocks + t, 1)
        points(blocks + t, 2)
        return 0

    lax.fori_loop(0, max(pairs, last_point // POINTS + 1 - blocks), drain, 0)

    for c in range(0, width, 128):
        cols = slice(c, c + 128)
        for b in range(images):
            dn_a[c // 128, pl.ds(b, patches, stride=images), :] = out_a[b * patches : (b + 1) * patches, cols]
        n2_f[:, cols] = dn_a[c // 128].astype(BF)
    own_out = pltpu.make_async_copy(n2_f, out_o, o_l.at[0])
    own_out.start()

    t_rows = t_b.shape[0] // n_mp
    v_rows = v_b.shape[0] // n_mp
    s_rows = t_s2.shape[0]
    t_b[...] = tg_a[...].astype(BF)
    w_v = v_b.shape[1]
    va[0:2, :] = ln1_a[...].T[0:2, :]
    for row in range(7):
        for c in range(width // w_v):
            v_b[row * 2 + c : row * 2 + c + 1, :] = va[row : row + 1, c * w_v : (c + 1) * w_v]
    for c in range(0, blocks * BLOCK, 128):
        row, col = 14 + c // w_v, c % w_v
        v_b[row : row + 1, col : col + 128] = cb1_a[c // BLOCK, 0:1, c % BLOCK : c % BLOCK + 128]

    sem = 0
    copies = []
    for k in range(1, n_mp):
        other, to = mp_peer(k)
        copies.append(
            remote(t_b.at[pl.ds(pl.multiple_of(other * t_rows, 16), t_rows)], t_r1.at[mp_me], sm_s.at[sem], sm_r.at[sem], to)
        )
        copies.append(
            remote(v_b.at[pl.ds(pl.multiple_of(other * v_rows, 8), v_rows)], v_r1.at[mp_me], sm_s.at[sem + 1], sm_r.at[sem + 1], to)
        )
        sem += 2
    for copy in copies:
        copy.start()
    t_r1[mp_me] = t_b[pl.ds(pl.multiple_of(mp_me * t_rows, 16), t_rows), :]
    v_r1[mp_me] = v_b[pl.ds(pl.multiple_of(mp_me * v_rows, 8), v_rows), :]
    for copy in copies:
        copy.wait()
    acc_t, acc_v = t_r1[0].astype(F32), v_r1[0]
    for k in range(1, n_mp):
        acc_t, acc_v = acc_t + t_r1[k].astype(F32), acc_v + v_r1[k]
    t_s1[...] = acc_t.astype(BF)
    v_s1[0] = acc_v

    def spot(i):
        return pl.ds(pl.multiple_of(i * s_rows, 16), s_rows)

    for g, group in enumerate(groups):
        size = group[1]
        mine = member(group)
        copies = []
        for k in range(1, size):
            other, to = peer(group, k)
            src = t_s1.at[spot(other)] if g == 0 else t_s2
            copies.append(remote(src, t_r2.at[g, mine], sm_s.at[sem], sm_r.at[sem], to))
            copies.append(remote(v_s1.at[g], v_r2.at[g, mine], sm_s.at[sem + 1], sm_r.at[sem + 1], to))
            sem += 2
        for copy in copies:
            copy.start()
        t_r2[g, mine] = t_s1[spot(mine)] if g == 0 else t_s2[...]
        v_r2[g, mine] = v_s1[g]
        for copy in copies:
            copy.wait()
        acc_t, acc_v = t_r2[g, 0].astype(F32), v_r2[g, 0]
        for k in range(1, size):
            acc_t, acc_v = acc_t + t_r2[g, k].astype(F32), acc_v + v_r2[g, k]
        t_s2[...] = acc_t.astype(BF)
        v_s1[g + 1] = acc_v

    group = groups[0]
    mine = member(group)
    v_sum = v_s1.at[len(groups)]
    v_here = smv_o.at[pl.ds(pl.multiple_of(mp_me * v_rows, 8), v_rows)]
    t_here = smt_o.at[pl.ds(pl.multiple_of(mp_me * t_rows, 16), t_rows)]
    copies, later = [], []
    for k in range(1, group[1]):
        _, to = peer(group, k)
        copies.append(remote(t_s2, t_g.at[spot(mine)], sm_s.at[sem], sm_r.at[sem], to))
        sem += 1
    for k in range(1, n_mp):
        _, to = mp_peer(k)
        later.append(remote(v_sum, v_here, sm_s.at[sem], sm_r.at[sem], to))
        sem += 1
    for copy in copies + later:
        copy.start()
    v_own = pltpu.make_async_copy(v_sum, v_here, sm_l.at[0])
    v_own.start()
    t_g[spot(mine)] = t_s2[...]
    for copy in copies:
        copy.wait()
    for k in range(1, n_mp):
        _, to = mp_peer(k)
        copy = remote(t_g, t_here, sm_s.at[sem], sm_r.at[sem], to)
        copy.start()
        later.append(copy)
        sem += 1
    t_own = pltpu.make_async_copy(t_g, t_here, sm_l.at[1])
    t_own.start()
    v_own.wait()
    t_own.wait()
    for copy in later:
        copy.wait()

    def wait_grads(b, _):
        for k in range(1, n_mp):
            other, to = mp_peer(k)
            grad_copy(k, b).wait_send()
            remote(
                x_in.at[b, channels(other)],
                dtok_o.at[other * images + b],
                out_s.at[k - 1, b],
                out_r.at[other, b],
                to,
            ).wait_recv()
        own_grad(b).wait()
        return 0

    lax.fori_loop(0, images, wait_grads, 0)
    own_out.wait()


def body(tokens, cot, g1, c1, tw1, tb1, tw2, tb2, g2, c2, w1, b1, w2, b2):
    n_mp, n_dp = lax.axis_size("mp"), lax.axis_size("dp")
    images, patches, width = cot.shape
    hidden = tw1.shape[1]
    local = tokens.shape[2]
    deep = w1.shape[1]
    tokens = tokens.transpose(0, 2, 1)
    cot = cot.transpose(1, 0, 2).reshape(patches * images, width)
    tw2 = tw2.T
    blocks = deep // BLOCK
    streams = reduce_plan(n_mp, n_dp, width)
    groups = dp_groups(n_dp)
    total = images * patches
    half_w = width // 2
    stage_rows = [(4 if t == 0 else blocks, have) for _, _, stages in streams for t, (_, have, _) in enumerate(stages)]
    n_ids = 1 + len(stage_rows)
    n_small = 2 * (n_mp - 1) + sum(2 * (size - 1) for _, size in groups) + groups[0][1] - 1 + 2 * (n_mp - 1)
    t_rows = 2 * SPACE // n_mp
    s_rows = t_rows // groups[0][1]
    hbm, vmem = pl.BlockSpec(memory_space=pl.ANY), pl.BlockSpec(memory_space=pltpu.VMEM)
    dma = pltpu.SemaphoreType.DMA
    scratch = [
        pltpu.VMEM((images, width, patches), BF),
        pltpu.VMEM((patches, width), BF),
        pltpu.VMEM((images, patches, width), BF),
        pltpu.VMEM((total, width), BF),
        pltpu.VMEM((width, total), BF),
        pltpu.VMEM((total, width), BF),
        pltpu.VMEM((width, total), BF),
        pltpu.VMEM((images, width, hidden), BF),
        pltpu.VMEM((images, width, hidden), BF),
        pltpu.VMEM((total, width), F32),
        pltpu.VMEM((width // 128, total, 128), F32),
        pltpu.VMEM((total, BLOCK), BF),
        pltpu.VMEM((total, BLOCK), BF),
        pltpu.VMEM((2, width, BLOCK), BF),
        pltpu.VMEM((2, BLOCK, width), BF),
        pltpu.VMEM((2, width, BLOCK), BF),
        pltpu.VMEM((SLOTS, width, BLOCK), BF),
        [pltpu.VMEM((min(keep, blocks), rows, BLOCK), BF) for keep, rows in stage_rows],
        pltpu.VMEM((width, SPACE), BF),
        pltpu.VMEM((SPACE, width), BF),
        pltpu.VMEM((width, SPACE), BF),
        pltpu.VMEM((SPACE, hidden), BF),
        pltpu.VMEM((hidden, SPACE), BF),
        pltpu.VMEM((hidden, SPACE), BF),
        pltpu.VMEM((SPACE, hidden), BF),
        pltpu.VMEM((8, width), F32),
        pltpu.VMEM((blocks, 8, BLOCK), F32),
        pltpu.VMEM((2, width, 128), F32),
        pltpu.VMEM((blocks, 8, BLOCK), F32),
        pltpu.VMEM((8, width), F32),
        pltpu.VMEM((width, 128), F32),
        pltpu.VMEM((2 * SPACE, hidden), F32),
        pltpu.VMEM((2 * SPACE, hidden), BF),
        pltpu.VMEM((n_mp, t_rows, hidden), BF),
        pltpu.VMEM((t_rows, hidden), BF),
        pltpu.VMEM((len(groups), groups[0][1], s_rows, hidden), BF),
        pltpu.VMEM((s_rows, hidden), BF),
        pltpu.VMEM((t_rows, hidden), BF),
        pltpu.VMEM((8 * n_mp, half_w), F32),
        pltpu.VMEM((n_mp, 8, half_w), F32),
        pltpu.VMEM((len(groups) + 1, 8, half_w), F32),
        pltpu.VMEM((len(groups), groups[0][1], 8, half_w), F32),
        dma((n_mp - 1, images)),
        dma((n_mp, images)),
        dma((images,)),
        dma((1,)),
        dma((2, 2)),
        dma((1,)),
        dma((n_mp - 1, images)),
        dma((n_mp, images)),
        dma((images,)),
        dma((n_ids, blocks)),
        dma((n_ids, blocks)),
        dma((n_ids, blocks)),
        dma((n_ids, blocks)),
        dma((len(streams), blocks)),
        dma((n_small,)),
        dma((n_small,)),
        dma((2,)),
    ]
    out, dtok, gw, smt, smv = pl.pallas_call(
        functools.partial(layer_kernel, n_mp, n_dp, streams, groups),
        out_shape=(
            jax.ShapeDtypeStruct(cot.shape, BF),
            jax.ShapeDtypeStruct(tokens.shape, BF),
            jax.ShapeDtypeStruct((2, width, deep), BF),
            jax.ShapeDtypeStruct((2 * SPACE, hidden), BF),
            jax.ShapeDtypeStruct((8 * n_mp, half_w), F32),
        ),
        in_specs=[hbm] * 4 + [vmem] * 10,
        out_specs=(hbm,) * 5,
        scratch_shapes=scratch,
        compiler_params=pltpu.CompilerParams(
            collective_id=0, has_side_effects=True, vmem_limit_bytes=64 * 2**20 - 2**16
        ),
    )(tokens, cot, w1, w2, g1, c1, tw1, tb1, tw2, tb2, g2, c2, b1, b2)
    vec = smv.reshape(-1)
    last = 7 * width
    return (
        out.reshape(patches, images, width).transpose(1, 0, 2),
        dtok.transpose(0, 2, 1),
        vec[0:width],
        vec[width : 2 * width],
        smt[0:patches].astype(F32),
        vec[5 * width : 5 * width + hidden],
        smt[SPACE : SPACE + patches].astype(F32).T,
        vec[6 * width : 6 * width + patches],
        vec[2 * width : 3 * width],
        vec[3 * width : 4 * width],
        gw[0].astype(F32),
        vec[last : last + deep],
        gw[1].T.astype(F32),
        vec[4 * width : 5 * width],
    )


def solution(mesh):
    placed = (P("dp", None, "mp"), P(("dp", "mp"), None, None)) + (P(),) * 12
    return jax.shard_map(body, mesh=mesh, in_specs=placed, out_specs=(placed[1], placed[0]) + (P(),) * 12, check_vma=False)
```

```python
import functools

import jax
import jax.numpy as jnp
from jax import lax
from jax.experimental import pallas as pl
from jax.experimental.pallas import tpu as pltpu
from jax.sharding import PartitionSpec as P

BF = jnp.bfloat16
F32 = jnp.float32
EPS = 1e-06
MESH = pl.DeviceIdType.MESH
NT = (((1,), (1,)), ((), ()))

BLOCK = 512
ROW = 200
VMEM_LIMIT = 64 * 2**20 - 2**16
SPACE = 256
PLAN = (
    (),
    (),
    (10000,),
    (),
    (10100, 20000, 30000, 40000),
    (),
    (10200, 20001, 30001, 40001, 20100, 40100),
    (30002, 30100, 20002),
    (10300, 40002, 20101, 40101, 20200, 30003, 40200, 20003, 30200),
    (40003, 30101),
    (10400, 20102, 30102, 40102, 20201, 30201, 40201, 20300, 30300, 20004, 30004, 40004),
    (20103, 40103, 40300, 30103, 30202),
    (10500, 20202, 20301, 20400, 30400, 30005, 40104, 40202, 40301, 20005),
    (20203, 30203, 40203, 20500, 40005, 20104, 30301, 20401, 30104),
    (40401, 30402, 20403, 20502, 20007, 20106, 20205, 30501, 30106, 40206, 20304, 30304),
    (20302, 40302, 30302, 30500, 20006, 30105, 40105, 40204),
    (40303, 20501, 40006, 20204, 30204),
    (20303, 30303, 40400, 30401, 20402, 30006, 20105, 40106, 40304),
    (30205, 40205),
    (40500, 30007, 20008, 40305),
    (30403, 20503, 30008, 20206, 30206, 30502, 20404),
    (40402, 40501, 40007, 30107, 20305, 30305, 40306),
    (30503, 40008, 40107, 30108, 30207, 30404, 20405, 20504),
    (40403, 40502, 40108, 40207, 30208, 20306, 30306, 20406, 30504, 20505),
    (40208, 40307, 30405, 20506),
    (40503, 20107, 30307, 40308, 40404),
    (30406, 20108, 30308, 30505, 40405, 40504, 30407, 30506, 40406, 30408, 40505, 20207, 30507, 20208, 40407, 40506, 30508, 40408, 40507, 20307, 20407, 20507, 40508, 20308, 20408, 20508),
)


def dot(a, b):
    return jnp.dot(a, b, preferred_element_type=F32)


def dot_nt(a, b):
    return lax.dot_general(a, b, NT, preferred_element_type=F32)


def gelu_both(v):
    cdf = 0.5 + 0.5 * lax.erf(v * 0.7071067811865476)
    return v * cdf, cdf + v * (jnp.exp(-0.5 * v * v) * 0.3989422804014327)


def standardize(v, axis):
    width = v.shape[axis]
    mean = jnp.sum(v, axis=axis, keepdims=True) / width
    square = jnp.sum(v * v, axis=axis, keepdims=True) / width
    rstd = lax.rsqrt(square - mean * mean + EPS)
    return (v - mean) * rstd, rstd


def bits_of(n):
    return n.bit_length() - 1


def reduce_plan(n_mp, n_dp, width):
    dp = [("dp", b) for b in range(bits_of(n_dp))]
    mp = [("mp", b) for b in range(1, bits_of(n_mp))]
    if len(dp) == 3 and len(mp) == 1:
        third = width // 3
        orders = ([mp[0], dp[0], dp[1], dp[2]], [dp[0], dp[1], mp[0], dp[2]], [dp[1], dp[0], dp[2], mp[0]])
        raw = [(s * third, third, order) for s, order in enumerate(orders)]
    else:
        raw = [(0, width, dp + mp)]
    streams = []
    for base, rows, keys in raw:
        stages, have = [], rows
        for key in keys:
            halved = have % 32 == 0
            have = have // 2 if halved else have
            stages.append((key, have, halved))
        streams.append((base, rows, stages))
    return streams


def small_groups(n_mp, n_dp):
    size = min(8, n_dp)
    groups, stride = [(1, size, n_mp // 2)], size
    while stride < n_dp:
        size = min(8, n_dp // stride)
        groups.append((stride, size, 1))
        stride *= size
    return groups


def plan_steps(blocks, images, streams):
    pieces = [("block", j, p) for j in range(blocks) for p in range(2)] + [("loop",)] + [("dense", h) for h in range(2)]
    pieces += [("image", b) for b in range(images)] + [("out", h) for h in range(2)] + [("end",)]
    if len(streams) == 3 and len(PLAN) == len(pieces) + 1:
        return dict(zip(pieces, PLAN)), PLAN[-1]
    table = {piece: [] for piece in pieces}
    for j in range(blocks):
        table[("block", j + 1, 0) if j + 1 < blocks else ("loop",)].append(10000 + 100 * j)
    last = max(len(stages) + sum(halved for _, _, halved in stages) for _, _, stages in streams)
    return table, [20000 + 10000 * s + 100 * j + k for k in range(last + 1) for j in range(blocks) for s in range(len(streams))]


def layer_kernel(
    n_mp,
    n_dp,
    streams,
    groups,
    tokens,
    cot,
    w1,
    w2,
    g1,
    c1,
    tw1,
    tb1,
    tw2,
    tb2,
    g2,
    c2,
    b1,
    b2,
    out_o,
    dtok_o,
    gw_o,
    smt_o,
    tok_h,
    hid_h,
    x_in,
    g_in,
    mid_p,
    g_f,
    n2_f,
    wide_s,
    tok_s,
    dn_a,
    dm_a,
    mix_s,
    hid_s,
    w1_s,
    w2_s,
    part,
    r0,
    rest,
    n1_s,
    dm_s,
    dm_t,
    tw1p,
    tw1t,
    tw2p,
    tw2t,
    rows_s,
    b1_s,
    cols_s,
    cb1_a,
    va,
    ln1_a,
    tg_a,
    t_b,
    t_r1,
    t_r2,
    t_s2,
    t_g,
    in_s,
    in_r,
    in_l,
    g_l,
    w_l,
    o_l,
    tok_l,
    hid_l,
    wide_l,
    out_s,
    out_r,
    out_l,
    rs_s,
    rs_r,
    ag_s,
    ag_r,
    own_l,
    sm_s,
    sm_r,
    sm_l,
):
    images, width, patches = x_in.shape
    local = tokens.shape[1]
    hidden = tw1.shape[1]
    blocks = w1.shape[1] // BLOCK
    total = images * patches
    half = total // 2
    mp_me = lax.axis_index("mp")
    dp_me = lax.axis_index("dp")

    def bit_of(key):
        axis, b = key
        me = mp_me if axis == "mp" else dp_me
        return (me // (1 << b)) % 2

    def partner(key):
        axis, b = key
        me = mp_me if axis == "mp" else dp_me
        return {axis: me + (1 << b) * (1 - 2 * bit_of(key))}

    def member(group):
        stride, size, across = group
        index = (dp_me // stride) % size
        return index * across + mp_me // 2 if across > 1 else index

    def peer(group, k):
        stride, size, across = group
        mine = member(group)
        other = lax.rem(mine + k, size * across)
        to = {"dp": dp_me + (other // across - (dp_me // stride) % size) * stride}
        if across > 1:
            to["mp"] = (other % across) * 2 + mp_me % 2
        return other, to

    def mp_peer(k):
        other = lax.rem(mp_me + k, n_mp)
        return other, {"mp": other}

    def remote(src, dst, send, recv, to):
        return pltpu.make_async_remote_copy(
            src_ref=src, dst_ref=dst, send_sem=send, recv_sem=recv, device_id=to, device_id_type=MESH
        )

    barrier = pltpu.get_barrier_semaphore()
    greet = [peer(group, k)[1] for group in groups for k in range(1, group[1] * group[2])]
    greet += [{"mp": (mp_me // 2 + k) % (n_mp // 2) * 2 + 1 - mp_me % 2} for k in range(n_mp // 2)]
    for to in greet:
        pl.semaphore_signal(barrier, inc=1, device_id=to, device_id_type=MESH)

    def channels(member):
        return pl.ds(pl.multiple_of(member * local, 16), local)

    def own_tokens(b):
        return pltpu.make_async_copy(tokens.at[mp_me * images + b], x_in.at[b, channels(mp_me)], in_l.at[b])

    own_cot = pltpu.make_async_copy(cot, n2_f, g_l.at[0])

    weights = (
        pltpu.make_async_copy(w1, w1_s, w_l.at[0]),
        pltpu.make_async_copy(w2, w2_s, w_l.at[1]),
    )

    def load_own(b, _):
        own_tokens(b).start()
        return 0

    own_cot.start()
    lax.fori_loop(0, images, load_own, 0)
    pl.semaphore_wait(barrier, len(greet))

    def token_copy(k, b):
        other, to = mp_peer(k)
        return remote(
            tokens.at[other * images + b], x_in.at[b, channels(mp_me)], in_s.at[k - 1, b], in_r.at[mp_me, b], to
        )

    def send_tokens(b, _):
        for k in range(1, n_mp):
            token_copy(k, b).start()
        return 0

    lax.fori_loop(0, images, send_tokens, 0)
    for copy in weights:
        copy.start()

    for row, ref in ((0, g1), (1, c1), (2, g2), (3, c2), (4, b2)):
        rows_s[row : row + 1, :] = ref[...].reshape(1, width)
    for j in range(blocks):
        b1_s[j, 0:1, :] = b1[j * BLOCK : (j + 1) * BLOCK].reshape(1, BLOCK)
    rows_s[5:6, 0:hidden] = tb1[...].reshape(1, hidden)
    rows_s[6:7, 0:patches] = tb2[...].reshape(1, patches)
    cols_s[0] = jnp.broadcast_to(rows_s[0:1, :], (128, width)).T
    cols_s[1] = jnp.broadcast_to(rows_s[1:2, :], (128, width)).T
    tw1p[...] = jnp.zeros_like(tw1p)
    tw1p[0:patches, :] = tw1[...]
    tw1t[...] = tw1p[...].T
    tw2t[...] = jnp.zeros_like(tw2t)
    tw2t[0:patches, :] = tw2[...]
    tw2p[...] = tw2t[...].T
    n1_s[...] = jnp.zeros_like(n1_s)
    dm_s[...] = jnp.zeros_like(dm_s)
    va[...] = jnp.zeros_like(va)
    ln1_a[...] = jnp.zeros_like(ln1_a)
    dm_t[...] = jnp.zeros_like(dm_t)
    tg_a[...] = jnp.zeros_like(tg_a)
    cb1_a[...] = jnp.zeros_like(cb1_a)

    own_cot.wait()
    for c in range(0, width, 128):
        cols = slice(c, c + 128)
        wide = n2_f[:, cols].astype(F32)
        va[4:5, cols] = jnp.sum(wide, axis=0, keepdims=True)
        mix_s[...] = wide
        for b in range(images):
            g_f[b * patches : (b + 1) * patches, cols] = mix_s[pl.ds(b, patches, stride=images), :].astype(BF)

    aside = -(-total // 128) * 128

    def transpose_rows(src, at):
        for lo in range(0, total, 128):
            hi = min(lo + 128, total)
            wide_s[0:width, at + lo : at + hi] = src[lo:hi, :].T

    transpose_rows(g_f, aside)

    def token_save(b):
        return pltpu.make_async_copy(tok_s.at[lax.rem(b, 2)], tok_h.at[b], tok_l.at[0, lax.rem(b, 2)])

    def token_load(b):
        return pltpu.make_async_copy(tok_h.at[b], tok_s.at[lax.rem(b, 2)], tok_l.at[1, lax.rem(b, 2)])

    def token_forward(b, _):
        for k in range(1, n_mp):
            other, to = mp_peer(k)
            remote(
                tokens.at[mp_me * images + b],
                x_in.at[b, channels(other)],
                in_s.at[k - 1, b],
                in_r.at[other, b],
                to,
            ).wait_recv()
        own_tokens(b).wait()
        x = x_in[b].astype(F32)
        xhat, _ = standardize(x, 0)
        n1_s[:, 0:patches] = (xhat * cols_s[0, :, 0:1] + cols_s[1, :, 0:1]).astype(BF)
        act, slope = gelu_both(dot(n1_s[...], tw1p[...]) + rows_s[5:6, 0:hidden])
        act = act.astype(BF)

        @pl.when(b >= 2)
        def _():
            token_save(b - 2).wait()

        slot = lax.rem(b, 2)
        tok_s[slot, 0] = act
        tok_s[slot, 1] = slope.astype(BF)
        token_save(b).start()
        mixed = dot(act, tw2p[...])[:, 0:patches] + rows_s[6:7, 0:patches]
        dm_t[:, 0:patches] = (x + mixed).astype(BF)
        mid_p[b] = dm_t[...].T[0:patches, :]
        return 0

    def second_norm(h):
        for b in range(h * images // 2, (h + 1) * images // 2):
            xhat, _ = standardize(mid_p[b].astype(F32), 1)
            n2_f[b * patches : (b + 1) * patches, :] = (xhat * rows_s[2:3, :] + rows_s[3:4, :]).astype(BF)

    def unit(h, j):
        slot = lax.rem(j, 2)
        rows = slice(h * half, (h + 1) * half)
        for lo in range(0, BLOCK, 256):
            here = pl.ds(pl.multiple_of(j * BLOCK + lo, 256), 256)
            cols = slice(lo, lo + 256)
            act, slope = gelu_both(dot(n2_f[rows, :], w1_s[:, here]) + b1_s[j, 0:1, cols])
            hid_s[slot, 0, rows, cols] = act.astype(BF)
            dp = dot_nt(g_f[rows, :], w2_s[here, :]) * slope
            cb1_a[j, 0:1, cols] += jnp.sum(dp, axis=0, keepdims=True)
            hid_s[slot, 1, rows, cols] = dp.astype(BF)

    def hidden_copies(kind, h, j):
        slot = lax.rem(j, 2)
        rows = pl.ds(h * half, half)
        cols = pl.ds(pl.multiple_of(j * BLOCK, BLOCK), BLOCK)
        pairs = [(hid_s.at[slot, i, rows, :], hid_h.at[i, rows, cols]) for i in range(2)]
        return [
            pltpu.make_async_copy(here if kind == 0 else there, there if kind == 0 else here, hid_l.at[kind, h, i, slot])
            for i, (here, there) in enumerate(pairs)
        ]

    def start(copies):
        for copy in copies:
            copy.start()

    def wait(copies):
        for copy in copies:
            copy.wait()

    lax.fori_loop(0, images // 2, token_forward, 0)
    second_norm(0)
    wait(weights)

    def early(j, _):
        @pl.when(j >= 2)
        def _():
            wait(hidden_copies(0, 0, j - 2))

        unit(0, j)
        start(hidden_copies(0, 0, j))

        @pl.when(j < images // 2)
        def _():
            token_forward(images // 2 + j, 0)

        return 0

    lax.fori_loop(0, blocks, early, 0)
    for j in range(blocks - 2, blocks):
        wait(hidden_copies(0, 0, j))
    start(hidden_copies(1, 0, 0))
    for b in range(images - 2, images):
        token_save(b).wait()
    second_norm(1)
    transpose_rows(n2_f, 0)

    core = ("mp", 0)
    core_bit = bit_of(core)

    ids = {}
    for s, (_, _, stages) in enumerate(streams):
        for t in range(len(stages)):
            ids[s, t] = 1 + len(ids)
    held = []
    for base, rows, stages in streams:
        line, off = [(base, rows)], base
        for key, have, halved in stages:
            off = off + bit_of(key) * have if halved else off
            line.append((off, have))
        held.append(line)

    def region(s, t):
        off, rows = held[s][t]
        return pl.ds(off if isinstance(off, int) else pl.multiple_of(off, 16), rows)

    def sums(s, t, j):
        return rest[ids[s, t] - 1].at[j]

    def source(s, t, j):
        base, _, _ = streams[s]
        return (r0.at[j], base) if t == 0 else (sums(s, t - 1, j), 0)

    def core_copy(j):
        return remote(part.at[1 - core_bit], r0.at[j], rs_s.at[0, j], rs_r.at[0, j], partner(core))

    def stage_copy(s, t, j):
        key, rows, halved = streams[s][2][t]
        ref, low = source(s, t, j)
        low = low + (1 - bit_of(key)) * rows if halved else low
        if not isinstance(low, int):
            low = pl.multiple_of(low, 16)
        i = ids[s, t]
        return remote(ref.at[pl.ds(low, rows)], sums(s, t, j), rs_s.at[i, j], rs_r.at[i, j], partner(key))

    def add_rows(dst, src, low, rows, into=None, at=0):
        chunk = next(c for c in (64, 48, 32, 16) if rows % c == 0)

        def step(i, _):
            here = pl.ds(pl.multiple_of(i * chunk, 16), chunk)
            there = pl.ds(pl.multiple_of(low + i * chunk, 16), chunk)
            result = (dst[here, :].astype(F32) + src[there, :].astype(F32)).astype(BF)
            if into is None:
                dst[here, :] = result
            else:
                into[pl.ds(pl.multiple_of(at + i * chunk, 16), chunk), :] = result
            return 0

        lax.fori_loop(0, rows // chunk, step, 0)

    def finish_core(j):
        core_copy(j).wait()
        add_rows(r0.at[j], part.at[core_bit], 0, width)

    def finish_stage(s, t, j):
        stage_copy(s, t, j).wait()
        key, rows, halved = streams[s][2][t]
        ref, low = source(s, t, j)
        low = low + bit_of(key) * rows if halved else low
        if t == n_rs - 1:
            add_rows(sums(s, t, j), ref, low, rows, r0.at[j], held[s][n_rs][0])
        else:
            add_rows(sums(s, t, j), ref, low, rows)

    gathers = [[t for t in reversed(range(len(stages))) if stages[t][2]] for _, _, stages in streams]

    def own_copy(s, j):
        base, rows, _ = streams[s]
        there = gw_o.at[core_bit, pl.ds(base, rows), pl.ds(j * BLOCK, BLOCK)]
        return pltpu.make_async_copy(r0.at[j, pl.ds(base, rows), :], there, own_l.at[s, j])

    def gather_copy(s, a, j):
        t = gathers[s][a]
        key = streams[s][2][t][0]
        here = r0.at[j, region(s, t + 1), :]
        i = ids[s, t]
        return remote(here, here, ag_s.at[i, j], ag_r.at[i, j], partner(key))

    def gather_core(s, j):
        base, rows, _ = streams[s]
        there = gw_o.at[core_bit, pl.ds(base, rows), pl.ds(j * BLOCK, BLOCK)]
        i = 1 + len(ids) + s
        return remote(r0.at[j, pl.ds(base, rows), :], there, ag_s.at[i, j], ag_r.at[i, j], partner(core))

    n_rs = len(streams[0][2])
    every = range(len(streams))

    def advance(item):
        s, j, k = item // 10000 - 2, item // 100 % 100, item % 100
        if s < 0:
            finish_core(j)
            for s in every:
                stage_copy(s, 0, j).start()
            return
        n_ag = len(gathers[s])
        if k < n_rs:
            finish_stage(s, k, j)
        elif k < n_rs + n_ag:
            gather_copy(s, k - n_rs, j).wait()
        else:
            gather_core(s, j).wait()
            own_copy(s, j).wait()
        k += 1
        if k < n_rs:
            stage_copy(s, k, j).start()
        elif k < n_rs + n_ag:
            gather_copy(s, k - n_rs, j).start()
        elif k == n_rs + n_ag:
            gather_core(s, j).start()
            own_copy(s, j).start()

    table, rest_steps = plan_steps(blocks, images, streams)

    def slot_steps(items):
        for item in items:
            advance(item)

    def block_step(j, _):
        wait(hidden_copies(1, 0, j))

        @pl.when(j >= 2)
        def _():
            wait(hidden_copies(0, 1, j - 2))

        unit(1, j)
        start(hidden_copies(0, 1, j))

        @pl.when(j + 1 < blocks)
        def _():
            start(hidden_copies(1, 0, j + 1))

        for k in range(blocks):
            if table["block", k, 0]:
                pl.when(j == k)(functools.partial(slot_steps, table["block", k, 0]))
        slot = lax.rem(j, 2)
        part[0] = dot(wide_s[0:width, 0:total], hid_s[slot, 1]).astype(BF)
        part[1] = dot(wide_s[0:width, aside : aside + total], hid_s[slot, 0]).astype(BF)
        core_copy(j).start()
        for k in range(blocks):
            if table["block", k, 1]:
                pl.when(j == k)(functools.partial(slot_steps, table["block", k, 1]))
        return 0

    lax.fori_loop(0, blocks, block_step, 0)
    slot_steps(table["loop",])
    for j in range(blocks - 2, blocks):
        wait(hidden_copies(0, 1, j))

    deep = blocks * BLOCK

    def wide_load(i, h):
        return pltpu.make_async_copy(hid_h.at[i, pl.ds(h * half, half)], wide_s.at[:, pl.ds(0, deep)], wide_l.at[i, h])

    wide_load(1, 0).start()
    token_load(0).start()

    def grad_copy(k, b):
        other, to = mp_peer(k)
        return remote(
            x_in.at[b, channels(other)], dtok_o.at[mp_me * images + b], out_s.at[k - 1, b], out_r.at[mp_me, b], to
        )

    def own_grad(b):
        return pltpu.make_async_copy(x_in.at[b, channels(mp_me)], dtok_o.at[mp_me * images + b], out_l.at[b])

    def token_backward(b, _):
        q = lax.rem(b, images // 2)

        @pl.when(b + 1 < images)
        def _():
            token_load(b + 1).start()

        xhat2, rstd2 = standardize(mid_p[b].astype(F32), 1)
        for i in range(images // 2):

            @pl.when(q == i)
            def _():
                quad = g_f.at[pl.ds(pl.multiple_of(half * (b // (images // 2)), 16), half)]
                g_in[...] = quad[i * patches : (i + 1) * patches, :]
                dm_a[...] = dn_a[i * patches : (i + 1) * patches, :]

        dn2 = dm_a[...]
        va[2:3, :] += jnp.sum(dn2 * xhat2, axis=0, keepdims=True)
        va[3:4, :] += jnp.sum(dn2, axis=0, keepdims=True)
        dxh = dn2 * rows_s[2:3, :]
        first = jnp.sum(dxh, axis=-1, keepdims=True) / width
        second = jnp.sum(dxh * xhat2, axis=-1, keepdims=True) / width
        dm_s[0:patches, :] = (g_in[...].astype(F32) + rstd2 * (dxh - first - xhat2 * second)).astype(BF)
        dm_t[...] = dm_s[...].T
        d_mid = dm_t[:, 0:patches].astype(F32)
        va[6:7, 0:patches] += jnp.sum(d_mid, axis=0, keepdims=True)
        token_load(b).wait()
        slot = lax.rem(b, 2)
        d_pre = dot(dm_t[...], tw2t[...]) * tok_s[slot, 1].astype(F32)
        va[5:6, 0:hidden] += jnp.sum(d_pre, axis=0, keepdims=True)
        d_pre = d_pre.astype(BF)
        tg_a[SPACE:, :] += dot(dm_s[...], tok_s[slot, 0])
        xhat1, rstd1 = standardize(x_in[b].astype(F32), 0)
        n1_s[:, 0:patches] = (xhat1 * cols_s[0, :, 0:1] + cols_s[1, :, 0:1]).astype(BF)
        tg_a[0:SPACE, :] += dot(n1_s[...].T, d_pre)
        dn1 = dot(d_pre, tw1t[...])[:, 0:patches]
        ln1_a[:, 0:1] += jnp.sum(dn1 * xhat1, axis=1, keepdims=True)
        ln1_a[:, 1:2] += jnp.sum(dn1, axis=1, keepdims=True)
        dxh = dn1 * cols_s[0, :, 0:1]
        first = jnp.sum(dxh, axis=0, keepdims=True) / width
        second = jnp.sum(dxh * xhat1, axis=0, keepdims=True) / width
        x_in[b] = (d_mid + rstd1 * (dxh - first - xhat1 * second)).astype(BF)
        for k in range(1, n_mp):
            grad_copy(k, b).start()
        own_grad(b).start()
        for k in range(images):
            if table["image", k]:
                pl.when(b == k)(functools.partial(slot_steps, table["image", k]))
        return 0

    def wait_tokens(b, _):
        for k in range(1, n_mp):
            token_copy(k, b).wait_send()
        return 0

    lax.fori_loop(0, images, wait_tokens, 0)

    for h in range(2):
        wide_load(1, h).wait()
        dn_a[...] = dot_nt(wide_s[:, 0:deep], w1_s[...])
        wide_load(*((1, 1) if h == 0 else (0, 0))).start()
        slot_steps(table["dense", h])
        lax.fori_loop(h * images // 2, (h + 1) * images // 2, token_backward, 0)

    group = groups[0]
    mine = member(group)
    t_half = t_b.shape[0] // 2
    s_rows = t_s2.shape[0]
    w_v = t_b.shape[1]
    va[0:2, :] = ln1_a[...].T[0:2, :]
    for row in range(7):
        for c in range(width // w_v):
            at = ROW + row * 2 + c
            tg_a[at : at + 1, :] = va[row : row + 1, c * w_v : (c + 1) * w_v]
    for c in range(0, deep, 128):
        at, col = ROW + 14 + c // w_v, c % w_v
        tg_a[at : at + 1, col : col + 128] = cb1_a[c // BLOCK, 0:1, c % BLOCK : c % BLOCK + 128]
    t_b[...] = tg_a[...].astype(BF)

    def spot(i):
        return pl.ds(pl.multiple_of(i * s_rows, 16), s_rows)

    def side(i):
        return pl.ds(pl.multiple_of(i * t_half, 16), t_half)

    sem = 0
    core_sum = remote(t_b.at[side(1 - core_bit)], t_r1, sm_s.at[0], sm_r.at[0], partner(core))
    sem += 1
    spread, back = [], []
    for g, team in enumerate(groups):
        copies = []
        for k in range(1, team[1] * team[2]):
            other, to = peer(team, k)
            src = t_r1.at[spot(other)] if g == 0 else t_s2
            copies.append(remote(src, t_r2.at[g, member(team)], sm_s.at[sem], sm_r.at[sem], to))
            sem += 1
        spread.append(copies)
    for k in range(1, group[1] * group[2]):
        _, to = peer(group, k)
        back.append(remote(t_s2, t_g.at[spot(mine)], sm_s.at[sem], sm_r.at[sem], to))
        sem += 1
    t_here = smt_o.at[side(core_bit)]
    core_back = remote(t_g, t_here, sm_s.at[sem], sm_r.at[sem], partner(core))
    own_small = pltpu.make_async_copy(t_g, t_here, sm_l.at[0])

    def sum_team(g):
        count = groups[g][1] * groups[g][2]
        acc = t_r2[g, 0].astype(F32)
        for k in range(1, count):
            acc = acc + t_r2[g, k].astype(F32)
        t_s2[...] = acc.astype(BF)

    core_sum.start()

    def out_rows(h):
        wide_load(0, h).wait()
        result = dot(wide_s[:, 0:deep], w2_s[...])
        for i in range(images // 2):
            b = h * images // 2 + i
            rows = result[i * patches : (i + 1) * patches, :]
            mid_p[b] = (mid_p[b].astype(F32) + rows + rows_s[4:5, :]).astype(BF)
        if h == 0:
            wide_load(0, 1).start()
        slot_steps(table["out", h])

    out_rows(0)
    core_sum.wait()
    t_r1[...] = (t_r1[...].astype(F32) + t_b[side(core_bit), :].astype(F32)).astype(BF)
    start(spread[0])
    t_r2[0, mine] = t_r1[spot(mine), :]
    out_rows(1)
    wait(spread[0])
    sum_team(0)
    for g in range(1, len(groups)):
        start(spread[g])
        t_r2[g, member(groups[g])] = t_s2[...]
        wait(spread[g])
        sum_team(g)
    start(back)
    t_g[spot(mine), :] = t_s2[...]

    for c in range(0, width, 128):
        cols = slice(c, c + 128)
        for b in range(images):
            mix_s[pl.ds(b, patches, stride=images), :] = mid_p[b, :, cols].astype(F32)
        n2_f[:, cols] = mix_s[...].astype(BF)
    own_out = pltpu.make_async_copy(n2_f, out_o, o_l.at[0])
    own_out.start()
    slot_steps(table["end",])
    wait(back)
    core_back.start()
    own_small.start()
    slot_steps(rest_steps)
    core_back.wait()
    own_small.wait()

    def wait_grads(b, _):
        for k in range(1, n_mp):
            other, to = mp_peer(k)
            grad_copy(k, b).wait_send()
            remote(
                x_in.at[b, channels(other)],
                dtok_o.at[other * images + b],
                out_s.at[k - 1, b],
                out_r.at[other, b],
                to,
            ).wait_recv()
        own_grad(b).wait()
        return 0

    lax.fori_loop(0, images, wait_grads, 0)
    own_out.wait()


def finish_kernel(
    out,
    dtok,
    gw,
    smt,
    out_o,
    dtok_o,
    g_ln1,
    b_ln1,
    g_tw1,
    g_tb1,
    g_tw2,
    g_tb2,
    g_ln2,
    b_ln2,
    g_cw1,
    g_cb1,
    g_cw2,
    g_cb2,
):
    @pl.when(pl.program_id(0) == 0)
    def _():
        patches, width = g_tw1.shape[0], g_ln1.shape[0]
        g_tw1[...] = smt[0:patches, :].astype(F32)
        g_tw2[...] = smt[SPACE : SPACE + patches, :].astype(F32)
        per = width // smt.shape[1]
        small = smt[ROW:SPACE, :].astype(F32)
        for row, ref in ((0, g_ln1), (1, b_ln1), (2, g_ln2), (3, b_ln2), (4, g_cb2), (5, g_tb1), (6, g_tb2), (7, g_cb1)):
            n = ref.shape[0]
            rows = [small[row * per + i : row * per + i + 1, :] for i in range(-(-n // smt.shape[1]))]
            ref[...] = jnp.concatenate(rows, axis=1)[:, 0:n].reshape(n)

    g_cw1[...] = gw[0].astype(F32)
    g_cw2[...] = gw[1].astype(F32).T
    out_o[...] = out[...]
    dtok_o[...] = dtok[...]


def body(tokens, cot, g1, c1, tw1, tb1, tw2, tb2, g2, c2, w1, b1, w2, b2):
    n_mp, n_dp = lax.axis_size("mp"), lax.axis_size("dp")
    images, patches, width = cot.shape
    hidden = tw1.shape[1]
    local = tokens.shape[2]
    deep = w1.shape[1]
    tokens = tokens.transpose(0, 2, 1)
    cot = cot.transpose(1, 0, 2).reshape(patches * images, width)
    tw2 = tw2.T
    blocks = deep // BLOCK
    streams = reduce_plan(n_mp, n_dp, width)
    groups = small_groups(n_mp, n_dp)
    total = images * patches
    stage_rows = [have for _, _, stages in streams for _, have, _ in stages]
    n_ids = 1 + len(stage_rows)
    team = groups[0][1] * groups[0][2]
    n_small = 2 + team - 1 + sum(size * across - 1 for _, size, across in groups)
    s_rows = SPACE // team
    hbm, vmem = pl.BlockSpec(memory_space=pl.ANY), pl.BlockSpec(memory_space=pltpu.VMEM)
    dma = pltpu.SemaphoreType.DMA
    scratch = [
        pltpu.VMEM((images, width, patches), BF),
        pltpu.VMEM((patches, width), BF),
        pltpu.VMEM((images, patches, width), BF),
        pltpu.VMEM((total, width), BF),
        pltpu.VMEM((total, width), BF),
        pltpu.VMEM((total // 2, max(deep, 2 * (-(-total // 128) * 128))), BF),
        pltpu.VMEM((2, 2, width, hidden), BF),
        pltpu.VMEM((total // 2, width), F32),
        pltpu.VMEM((patches, width), F32),
        pltpu.VMEM((total, 128), F32),
        pltpu.VMEM((2, 2, total, BLOCK), BF),
        pltpu.VMEM((width, deep), BF),
        pltpu.VMEM((deep, width), BF),
        pltpu.VMEM((2, width, BLOCK), BF),
        pltpu.VMEM((blocks, width, BLOCK), BF),
        [pltpu.VMEM((blocks, rows, BLOCK), BF) for rows in stage_rows],
        pltpu.VMEM((width, SPACE), BF),
        pltpu.VMEM((SPACE, width), BF),
        pltpu.VMEM((width, SPACE), BF),
        pltpu.VMEM((SPACE, hidden), BF),
        pltpu.VMEM((hidden, SPACE), BF),
        pltpu.VMEM((hidden, SPACE), BF),
        pltpu.VMEM((SPACE, hidden), BF),
        pltpu.VMEM((8, width), F32),
        pltpu.VMEM((blocks, 8, BLOCK), F32),
        pltpu.VMEM((2, width, 128), F32),
        pltpu.VMEM((blocks, 8, BLOCK), F32),
        pltpu.VMEM((8, width), F32),
        pltpu.VMEM((width, 128), F32),
        pltpu.VMEM((2 * SPACE, hidden), F32),
        pltpu.VMEM((2 * SPACE, hidden), BF),
        pltpu.VMEM((SPACE, hidden), BF),
        pltpu.VMEM((len(groups), team, s_rows, hidden), BF),
        pltpu.VMEM((s_rows, hidden), BF),
        pltpu.VMEM((SPACE, hidden), BF),
        dma((n_mp - 1, images)),
        dma((n_mp, images)),
        dma((images,)),
        dma((1,)),
        dma((2,)),
        dma((1,)),
        dma((2, 2)),
        dma((2, 2, 2, 2)),
        dma((2, 2)),
        dma((n_mp - 1, images)),
        dma((n_mp, images)),
        dma((images,)),
        dma((n_ids, blocks)),
        dma((n_ids, blocks)),
        dma((n_ids + len(streams), blocks)),
        dma((n_ids + len(streams), blocks)),
        dma((len(streams), blocks)),
        dma((n_small,)),
        dma((n_small,)),
        dma((1,)),
    ]
    out, dtok, gw, smt, _, _ = pl.pallas_call(
        functools.partial(layer_kernel, n_mp, n_dp, streams, groups),
        out_shape=(
            jax.ShapeDtypeStruct(cot.shape, BF),
            jax.ShapeDtypeStruct(tokens.shape, BF),
            jax.ShapeDtypeStruct((2, width, deep), BF),
            jax.ShapeDtypeStruct((2 * SPACE, hidden), BF),
            jax.ShapeDtypeStruct((images, 2, width, hidden), BF),
            jax.ShapeDtypeStruct((2, total, deep), BF),
        ),
        in_specs=[hbm] * 4 + [vmem] * 10,
        out_specs=(hbm,) * 6,
        scratch_shapes=scratch,
        compiler_params=pltpu.CompilerParams(
            collective_id=0, has_side_effects=True, vmem_limit_bytes=VMEM_LIMIT
        ),
    )(tokens, cot, w1, w2, g1, c1, tw1, tb1, tw2, tb2, g2, c2, b1, b2)
    full = lambda n: jax.ShapeDtypeStruct((n,), F32)
    out_spec = pl.BlockSpec((total, width // blocks), lambda j: (0, j))
    dtok_spec = pl.BlockSpec((n_mp * images, local // blocks, patches), lambda j: (0, j, 0))
    results = pl.pallas_call(
        finish_kernel,
        grid=(blocks,),
        out_shape=(
            jax.ShapeDtypeStruct(out.shape, BF),
            jax.ShapeDtypeStruct(dtok.shape, BF),
            full(width),
            full(width),
            jax.ShapeDtypeStruct((patches, hidden), F32),
            full(hidden),
            jax.ShapeDtypeStruct((patches, hidden), F32),
            full(patches),
            full(width),
            full(width),
            jax.ShapeDtypeStruct((width, deep), F32),
            full(deep),
            jax.ShapeDtypeStruct((deep, width), F32),
            full(width),
        ),
        in_specs=[out_spec, dtok_spec, pl.BlockSpec((2, width, BLOCK), lambda j: (0, 0, j)), vmem],
        out_specs=(
            (out_spec, dtok_spec)
            + (vmem,) * 8
            + (
                pl.BlockSpec((width, BLOCK), lambda j: (0, j)),
                vmem,
                pl.BlockSpec((BLOCK, width), lambda j: (j, 0)),
                vmem,
            )
        ),
        compiler_params=pltpu.CompilerParams(vmem_limit_bytes=VMEM_LIMIT),
    )(out, dtok, gw, smt)
    out, dtok, *grads = results
    grads[4] = grads[4].T
    return (out.reshape(patches, images, width).transpose(1, 0, 2), dtok.transpose(0, 2, 1), *grads)


def solution(mesh):
    placed = (P("dp", None, "mp"), P(("dp", "mp"), None, None)) + (P(),) * 12
    return jax.shard_map(body, mesh=mesh, in_specs=placed, out_specs=(placed[1], placed[0]) + (P(),) * 12, check_vma=False)
```

```python
import functools

import jax
import jax.numpy as jnp
from jax import lax
from jax.experimental import pallas as pl
from jax.experimental.pallas import tpu as pltpu
from jax.sharding import PartitionSpec as P

BF = jnp.bfloat16
F32 = jnp.float32
EPS = 1e-06
MESH = pl.DeviceIdType.MESH
NT = (((1,), (1,)), ((), ()))

BLOCK = 512
ROW = 200
VMEM_LIMIT = 64 * 2**20 - 2**16
SPACE = 256
PLAN = (
    (),
    (),
    (10000,),
    (),
    (10100,),
    (20000, 30000, 40000),
    (10200,),
    (30001, 20100, 30100, 40100, 20001),
    (10300, 40001),
    (20002, 30002, 20101, 30101, 20200, 40101, 30200, 40200),
    (10400, 40002, 20300, 30300, 40300),
    (20003, 30003, 20102, 30102, 40102, 20201, 30201, 40201),
    (10500, 40003),
    (20303, 30303, 40303, 20402, 30402, 40402, 30501, 40005, 20006, 40105, 20204, 30204, 20502, 40204, 30105, 20105, 40502),
    (40103, 20301, 30301, 40301, 30202, 20400, 30400, 40400, 20004),
    (20103, 30103, 20202, 40202, 20500, 30500, 30004, 40004, 40104, 40500),
    (30203, 20302, 30302, 40302, 20401, 30401, 40401, 20005),
    (20203, 40203, 20501, 40501, 30005, 20104, 30104),
    (30006,),
    (40403, 20403, 30403, 30502, 40503, 40006, 20503, 30205, 40106, 20205, 20304, 20106, 40205, 30304, 30106, 40304),
    (20007, 30007),
    (30503, 20404, 30404, 40404, 20504, 40504),
    (20008, 30008, 30107, 20206, 30206, 40206, 20305, 30305, 40305),
    (40007, 20107, 40107, 30108, 20405, 30405, 40405, 30504, 20505, 40505),
    (40207, 20306, 30306, 40306),
    (40008, 20108, 40108, 20207, 30207, 40208, 30406, 30505, 20208, 30208, 20406, 40406, 20307, 20506, 40506, 20308, 30506, 40307, 40308, 20407, 20408, 30307, 20507, 30407, 40407, 40507, 30507, 30308, 30408, 20508, 40408, 40508, 30508),
)


def dot(a, b):
    return jnp.dot(a, b, preferred_element_type=F32)


def dot_nt(a, b):
    return lax.dot_general(a, b, NT, preferred_element_type=F32)


def gelu_both(v):
    cdf = 0.5 + 0.5 * lax.erf(v * 0.7071067811865476)
    return v * cdf, cdf + v * (jnp.exp(-0.5 * v * v) * 0.3989422804014327)


def standardize(v, axis):
    width = v.shape[axis]
    mean = jnp.sum(v, axis=axis, keepdims=True) / width
    square = jnp.sum(v * v, axis=axis, keepdims=True) / width
    rstd = lax.rsqrt(square - mean * mean + EPS)
    return (v - mean) * rstd, rstd


def bits_of(n):
    return n.bit_length() - 1


def reduce_plan(n_mp, n_dp, width):
    dp = [("dp", b) for b in range(bits_of(n_dp))]
    mp = [("mp", b) for b in range(1, bits_of(n_mp))]
    if len(dp) == 3 and len(mp) == 1:
        third = width // 3
        orders = ([mp[0], dp[0], dp[1], dp[2]], [dp[0], dp[1], mp[0], dp[2]], [dp[1], dp[0], dp[2], mp[0]])
        raw = [(s * third, third, order) for s, order in enumerate(orders)]
    else:
        raw = [(0, width, dp + mp)]
    streams = []
    for base, rows, keys in raw:
        stages, have = [], rows
        for key in keys:
            halved = have % 32 == 0
            have = have // 2 if halved else have
            stages.append((key, have, halved))
        streams.append((base, rows, stages))
    return streams


def small_groups(n_mp, n_dp):
    size = min(8, n_dp)
    groups, stride = [(1, size, n_mp // 2)], size
    while stride < n_dp:
        size = min(8, n_dp // stride)
        groups.append((stride, size, 1))
        stride *= size
    return groups


def plan_steps(blocks, images, streams):
    pieces = [("block", j, p) for j in range(blocks) for p in range(2)] + [("loop",), ("dense",)]
    pieces += [("image", b) for b in range(images)] + [("out", h) for h in range(2)] + [("end",)]
    if len(streams) == 3 and len(PLAN) == len(pieces) + 1:
        return dict(zip(pieces, PLAN)), PLAN[-1]
    table = {piece: [] for piece in pieces}
    for j in range(blocks):
        table[("block", j + 1, 0) if j + 1 < blocks else ("loop",)].append(10000 + 100 * j)
    last = max(len(stages) + sum(halved for _, _, halved in stages) for _, _, stages in streams)
    return table, [20000 + 10000 * s + 100 * j + k for k in range(last + 1) for j in range(blocks) for s in range(len(streams))]


def layer_kernel(
    n_mp,
    n_dp,
    streams,
    groups,
    tokens,
    cot,
    w1,
    w2,
    g1,
    c1,
    tw1,
    tb1,
    tw2,
    tb2,
    g2,
    c2,
    b1,
    b2,
    out_o,
    dtok_o,
    gw_o,
    smt_o,
    tok_h,
    hid_h,
    x_in,
    g_in,
    mid_p,
    g_f,
    n2_f,
    wide_s,
    tok_s,
    dn_a,
    dm_a,
    mix_s,
    hid_s,
    w1_s,
    w2_s,
    part,
    r0,
    rest,
    n1_s,
    dm_s,
    dm_t,
    tw1p,
    tw1t,
    tw2p,
    tw2t,
    rows_s,
    b1_s,
    cols_s,
    cb1_a,
    va,
    ln1_a,
    tg_a,
    t_b,
    t_r1,
    t_r2,
    t_s2,
    t_g,
    in_s,
    in_r,
    in_l,
    g_l,
    w_l,
    o_l,
    tok_l,
    hid_l,
    wide_l,
    out_s,
    out_r,
    out_l,
    rs_s,
    rs_r,
    ag_s,
    ag_r,
    own_l,
    sm_s,
    sm_r,
    sm_l,
):
    images, width, patches = x_in.shape
    local = tokens.shape[1]
    hidden = tw1.shape[1]
    blocks = w1.shape[1] // BLOCK
    total = images * patches
    half = total // 2
    mp_me = lax.axis_index("mp")
    dp_me = lax.axis_index("dp")

    def bit_of(key):
        axis, b = key
        me = mp_me if axis == "mp" else dp_me
        return (me // (1 << b)) % 2

    def partner(key):
        axis, b = key
        me = mp_me if axis == "mp" else dp_me
        return {axis: me + (1 << b) * (1 - 2 * bit_of(key))}

    def member(group):
        stride, size, across = group
        index = (dp_me // stride) % size
        return index * across + mp_me // 2 if across > 1 else index

    def peer(group, k):
        stride, size, across = group
        mine = member(group)
        other = lax.rem(mine + k, size * across)
        to = {"dp": dp_me + (other // across - (dp_me // stride) % size) * stride}
        if across > 1:
            to["mp"] = (other % across) * 2 + mp_me % 2
        return other, to

    def mp_peer(k):
        other = lax.rem(mp_me + k, n_mp)
        return other, {"mp": other}

    def remote(src, dst, send, recv, to):
        return pltpu.make_async_remote_copy(
            src_ref=src, dst_ref=dst, send_sem=send, recv_sem=recv, device_id=to, device_id_type=MESH
        )

    barrier = pltpu.get_barrier_semaphore()
    greet = [peer(group, k)[1] for group in groups for k in range(1, group[1] * group[2])]
    greet += [{"mp": (mp_me // 2 + k) % (n_mp // 2) * 2 + 1 - mp_me % 2} for k in range(n_mp // 2)]
    for to in greet:
        pl.semaphore_signal(barrier, inc=1, device_id=to, device_id_type=MESH)

    def channels(member):
        return pl.ds(pl.multiple_of(member * local, 16), local)

    def own_tokens(b):
        return pltpu.make_async_copy(tokens.at[mp_me * images + b], x_in.at[b, channels(mp_me)], in_l.at[b])

    own_cot = pltpu.make_async_copy(cot, n2_f, g_l.at[0])

    weights = (
        pltpu.make_async_copy(w1, w1_s, w_l.at[0]),
        pltpu.make_async_copy(w2, w2_s, w_l.at[1]),
    )

    def load_own(b, _):
        own_tokens(b).start()
        return 0

    own_cot.start()
    lax.fori_loop(0, images, load_own, 0)
    pl.semaphore_wait(barrier, len(greet))

    def token_copy(k, b):
        other, to = mp_peer(k)
        return remote(
            tokens.at[other * images + b], x_in.at[b, channels(mp_me)], in_s.at[k - 1, b], in_r.at[mp_me, b], to
        )

    def send_tokens(b, _):
        for k in range(1, n_mp):
            token_copy(k, b).start()
        return 0

    lax.fori_loop(0, images, send_tokens, 0)
    for copy in weights:
        copy.start()

    for row, ref in ((0, g1), (1, c1), (2, g2), (3, c2), (4, b2)):
        rows_s[row : row + 1, :] = ref[...].reshape(1, width)
    for j in range(blocks):
        b1_s[j, 0:1, :] = b1[j * BLOCK : (j + 1) * BLOCK].reshape(1, BLOCK)
    rows_s[5:6, 0:hidden] = tb1[...].reshape(1, hidden)
    rows_s[6:7, 0:patches] = tb2[...].reshape(1, patches)
    cols_s[0] = jnp.broadcast_to(rows_s[0:1, :], (128, width)).T
    cols_s[1] = jnp.broadcast_to(rows_s[1:2, :], (128, width)).T
    tw1p[...] = jnp.zeros_like(tw1p)
    tw1p[0:patches, :] = tw1[...]
    tw1t[...] = tw1p[...].T
    tw2t[...] = jnp.zeros_like(tw2t)
    tw2t[0:patches, :] = tw2[...]
    tw2p[...] = tw2t[...].T
    n1_s[...] = jnp.zeros_like(n1_s)
    dm_s[...] = jnp.zeros_like(dm_s)
    va[...] = jnp.zeros_like(va)
    ln1_a[...] = jnp.zeros_like(ln1_a)
    dm_t[...] = jnp.zeros_like(dm_t)
    tg_a[...] = jnp.zeros_like(tg_a)
    cb1_a[...] = jnp.zeros_like(cb1_a)

    own_cot.wait()
    for c in range(0, width, 128):
        cols = slice(c, c + 128)
        wide = n2_f[:, cols].astype(F32)
        va[4:5, cols] = jnp.sum(wide, axis=0, keepdims=True)
        mix_s[...] = wide
        for b in range(images):
            g_f[b * patches : (b + 1) * patches, cols] = mix_s[pl.ds(b, patches, stride=images), :].astype(BF)

    aside = -(-total // 128) * 128

    def transpose_rows(src, at, first=0, last=total):
        for lo in range(first, last, 128):
            hi = min(lo + 128, total)
            wide_s[0:width, at + lo : at + hi] = src[lo:hi, :].T

    transpose_rows(g_f, aside)

    def token_save(b):
        return pltpu.make_async_copy(tok_s.at[lax.rem(b, 2)], tok_h.at[b], tok_l.at[0, lax.rem(b, 2)])

    def token_load(b):
        return pltpu.make_async_copy(tok_h.at[b], tok_s.at[lax.rem(b, 2)], tok_l.at[1, lax.rem(b, 2)])

    def token_forward(b, _):
        for k in range(1, n_mp):
            other, to = mp_peer(k)
            remote(
                tokens.at[mp_me * images + b],
                x_in.at[b, channels(other)],
                in_s.at[k - 1, b],
                in_r.at[other, b],
                to,
            ).wait_recv()
        own_tokens(b).wait()
        x = x_in[b].astype(F32)
        xhat, _ = standardize(x, 0)
        n1_s[:, 0:patches] = (xhat * cols_s[0, :, 0:1] + cols_s[1, :, 0:1]).astype(BF)
        act, slope = gelu_both(dot(n1_s[...], tw1p[...]) + rows_s[5:6, 0:hidden])
        act = act.astype(BF)

        @pl.when(b >= 2)
        def _():
            token_save(b - 2).wait()

        slot = lax.rem(b, 2)
        tok_s[slot, 0] = act
        tok_s[slot, 1] = slope.astype(BF)
        token_save(b).start()
        mixed = dot(act, tw2p[...])[:, 0:patches] + rows_s[6:7, 0:patches]
        dm_t[:, 0:patches] = (x + mixed).astype(BF)
        mid_p[b] = dm_t[...].T[0:patches, :]
        return 0

    def second_norm(first, last):
        for b in range(first, last):
            xhat, _ = standardize(mid_p[b].astype(F32), 1)
            n2_f[b * patches : (b + 1) * patches, :] = (xhat * rows_s[2:3, :] + rows_s[3:4, :]).astype(BF)

    def unit(h, j):
        slot = lax.rem(j, 2)
        rows = slice(h * half, (h + 1) * half)
        for lo in range(0, BLOCK, 256):
            here = pl.ds(pl.multiple_of(j * BLOCK + lo, 256), 256)
            cols = slice(lo, lo + 256)
            act, slope = gelu_both(dot(n2_f[rows, :], w1_s[:, here]) + b1_s[j, 0:1, cols])
            hid_s[slot, 0, rows, cols] = act.astype(BF)
            dp = dot_nt(g_f[rows, :], w2_s[here, :]) * slope
            cb1_a[j, 0:1, cols] += jnp.sum(dp, axis=0, keepdims=True)
            hid_s[slot, 1, rows, cols] = dp.astype(BF)

    def hidden_copies(kind, h, j):
        slot = lax.rem(j, 2)
        rows = pl.ds(h * half, half)
        cols = pl.ds(pl.multiple_of(j * BLOCK, BLOCK), BLOCK)
        pairs = [(hid_s.at[slot, i, rows, :], hid_h.at[i, rows, cols]) for i in range(2)]
        return [
            pltpu.make_async_copy(here if kind == 0 else there, there if kind == 0 else here, hid_l.at[kind, h, i, slot])
            for i, (here, there) in enumerate(pairs)
        ]

    def start(copies):
        for copy in copies:
            copy.start()

    def wait(copies):
        for copy in copies:
            copy.wait()

    lax.fori_loop(0, images // 2, token_forward, 0)
    second_norm(0, images // 2)
    wait(weights)

    def early(j, _):
        @pl.when(j >= 2)
        def _():
            wait(hidden_copies(0, 0, j - 2))

        unit(0, j)
        start(hidden_copies(0, 0, j))
        cols = pl.ds(pl.multiple_of(j * BLOCK, BLOCK), BLOCK)
        dn_a[...] += dot_nt(hid_s[lax.rem(j, 2), 1, 0:half, :], w1_s[:, cols])

        @pl.when((j % 2 == 1) & (j < images - 4))
        def _():
            token_forward(images // 2 + j // 2, 0)

        return 0

    dn_a[...] = jnp.zeros_like(dn_a)
    lax.fori_loop(0, blocks, early, 0)
    for j in range(blocks - 2, blocks):
        wait(hidden_copies(0, 0, j))
    start(hidden_copies(1, 0, 0))
    lax.fori_loop(images - 2, images - 1, token_forward, 0)
    second_norm(images // 2, images - 1)
    ahead = (images - 1) * patches // 128 * 128
    transpose_rows(n2_f, 0, 0, ahead)
    lax.fori_loop(images - 1, images, token_forward, 0)
    for b in range(images - 2, images):
        token_save(b).wait()
    second_norm(images - 1, images)
    transpose_rows(n2_f, 0, ahead)

    core = ("mp", 0)
    core_bit = bit_of(core)

    ids = {}
    for s, (_, _, stages) in enumerate(streams):
        for t in range(len(stages)):
            ids[s, t] = 1 + len(ids)
    held = []
    for base, rows, stages in streams:
        line, off = [(base, rows)], base
        for key, have, halved in stages:
            off = off + bit_of(key) * have if halved else off
            line.append((off, have))
        held.append(line)

    def region(s, t):
        off, rows = held[s][t]
        return pl.ds(off if isinstance(off, int) else pl.multiple_of(off, 16), rows)

    def sums(s, t, j):
        return rest[ids[s, t] - 1].at[j]

    def source(s, t, j):
        base, _, _ = streams[s]
        return (r0.at[j], base) if t == 0 else (sums(s, t - 1, j), 0)

    def core_copy(j):
        return remote(part.at[1 - core_bit], r0.at[j], rs_s.at[0, j], rs_r.at[0, j], partner(core))

    def stage_copy(s, t, j):
        key, rows, halved = streams[s][2][t]
        ref, low = source(s, t, j)
        low = low + (1 - bit_of(key)) * rows if halved else low
        if not isinstance(low, int):
            low = pl.multiple_of(low, 16)
        i = ids[s, t]
        return remote(ref.at[pl.ds(low, rows)], sums(s, t, j), rs_s.at[i, j], rs_r.at[i, j], partner(key))

    def add_rows(dst, src, low, rows, into=None, at=0):
        chunk = next(c for c in (64, 48, 32, 16) if rows % c == 0)

        def step(i, _):
            here = pl.ds(pl.multiple_of(i * chunk, 16), chunk)
            there = pl.ds(pl.multiple_of(low + i * chunk, 16), chunk)
            result = dst[here, :] + src[there, :]
            if into is None:
                dst[here, :] = result
            else:
                into[pl.ds(pl.multiple_of(at + i * chunk, 16), chunk), :] = result
            return 0

        lax.fori_loop(0, rows // chunk, step, 0)

    def finish_core(j):
        core_copy(j).wait()
        add_rows(r0.at[j], part.at[core_bit], 0, width)

    def finish_stage(s, t, j):
        stage_copy(s, t, j).wait()
        key, rows, halved = streams[s][2][t]
        ref, low = source(s, t, j)
        low = low + bit_of(key) * rows if halved else low
        if t == n_rs - 1:
            add_rows(sums(s, t, j), ref, low, rows, r0.at[j], held[s][n_rs][0])
        else:
            add_rows(sums(s, t, j), ref, low, rows)

    gathers = [[t for t in reversed(range(len(stages))) if stages[t][2]] for _, _, stages in streams]

    def own_copy(s, j):
        base, rows, _ = streams[s]
        there = gw_o.at[core_bit, pl.ds(base, rows), pl.ds(j * BLOCK, BLOCK)]
        return pltpu.make_async_copy(r0.at[j, pl.ds(base, rows), :], there, own_l.at[s, j])

    def gather_copy(s, a, j):
        t = gathers[s][a]
        key = streams[s][2][t][0]
        here = r0.at[j, region(s, t + 1), :]
        i = ids[s, t]
        return remote(here, here, ag_s.at[i, j], ag_r.at[i, j], partner(key))

    def gather_core(s, j):
        base, rows, _ = streams[s]
        there = gw_o.at[core_bit, pl.ds(base, rows), pl.ds(j * BLOCK, BLOCK)]
        i = 1 + len(ids) + s
        return remote(r0.at[j, pl.ds(base, rows), :], there, ag_s.at[i, j], ag_r.at[i, j], partner(core))

    n_rs = len(streams[0][2])
    every = range(len(streams))

    def advance(item):
        s, j, k = item // 10000 - 2, item // 100 % 100, item % 100
        if s < 0:
            finish_core(j)
            for s in every:
                stage_copy(s, 0, j).start()
            return
        n_ag = len(gathers[s])
        if k < n_rs:
            finish_stage(s, k, j)
        elif k < n_rs + n_ag:
            gather_copy(s, k - n_rs, j).wait()
        else:
            gather_core(s, j).wait()
            own_copy(s, j).wait()
        k += 1
        if k < n_rs:
            stage_copy(s, k, j).start()
        elif k < n_rs + n_ag:
            gather_copy(s, k - n_rs, j).start()
        elif k == n_rs + n_ag:
            gather_core(s, j).start()
            own_copy(s, j).start()

    table, rest_steps = plan_steps(blocks, images, streams)

    def slot_steps(items):
        for item in items:
            advance(item)

    def block_step(j, _):
        wait(hidden_copies(1, 0, j))

        @pl.when(j >= 2)
        def _():
            wait(hidden_copies(0, 1, j - 2))

        unit(1, j)
        start(hidden_copies(0, 1, j))

        @pl.when(j + 1 < blocks)
        def _():
            start(hidden_copies(1, 0, j + 1))

        for k in range(blocks):
            if table["block", k, 0]:
                pl.when(j == k)(functools.partial(slot_steps, table["block", k, 0]))
        slot = lax.rem(j, 2)
        part[0] = dot(wide_s[0:width, 0:total], hid_s[slot, 1]).astype(BF)
        part[1] = dot(wide_s[0:width, aside : aside + total], hid_s[slot, 0]).astype(BF)
        core_copy(j).start()
        for k in range(blocks):
            if table["block", k, 1]:
                pl.when(j == k)(functools.partial(slot_steps, table["block", k, 1]))
        return 0

    lax.fori_loop(0, blocks, block_step, 0)
    slot_steps(table["loop",])
    for j in range(blocks - 2, blocks):
        wait(hidden_copies(0, 1, j))

    deep = blocks * BLOCK

    def wide_load(i, h):
        return pltpu.make_async_copy(hid_h.at[i, pl.ds(h * half, half)], wide_s.at[:, pl.ds(0, deep)], wide_l.at[i, h])

    wide_load(1, 1).start()
    token_load(0).start()

    def grad_copy(k, b):
        other, to = mp_peer(k)
        return remote(
            x_in.at[b, channels(other)], dtok_o.at[mp_me * images + b], out_s.at[k - 1, b], out_r.at[mp_me, b], to
        )

    def own_grad(b):
        return pltpu.make_async_copy(x_in.at[b, channels(mp_me)], dtok_o.at[mp_me * images + b], out_l.at[b])

    def token_backward(b, _):
        q = lax.rem(b, images // 2)

        @pl.when(b + 1 < images)
        def _():
            token_load(b + 1).start()

        xhat2, rstd2 = standardize(mid_p[b].astype(F32), 1)
        for i in range(images // 2):

            @pl.when(q == i)
            def _():
                quad = g_f.at[pl.ds(pl.multiple_of(half * (b // (images // 2)), 16), half)]
                g_in[...] = quad[i * patches : (i + 1) * patches, :]
                dm_a[...] = dn_a[i * patches : (i + 1) * patches, :]

        dn2 = dm_a[...]
        va[2:3, :] += jnp.sum(dn2 * xhat2, axis=0, keepdims=True)
        va[3:4, :] += jnp.sum(dn2, axis=0, keepdims=True)
        dxh = dn2 * rows_s[2:3, :]
        first = jnp.sum(dxh, axis=-1, keepdims=True) / width
        second = jnp.sum(dxh * xhat2, axis=-1, keepdims=True) / width
        dm_s[0:patches, :] = (g_in[...].astype(F32) + rstd2 * (dxh - first - xhat2 * second)).astype(BF)
        dm_t[...] = dm_s[...].T
        d_mid = dm_t[:, 0:patches].astype(F32)
        va[6:7, 0:patches] += jnp.sum(d_mid, axis=0, keepdims=True)
        token_load(b).wait()
        slot = lax.rem(b, 2)
        d_pre = dot(dm_t[...], tw2t[...]) * tok_s[slot, 1].astype(F32)
        va[5:6, 0:hidden] += jnp.sum(d_pre, axis=0, keepdims=True)
        d_pre = d_pre.astype(BF)
        tg_a[SPACE:, :] += dot(dm_s[...], tok_s[slot, 0])
        xhat1, rstd1 = standardize(x_in[b].astype(F32), 0)
        n1_s[:, 0:patches] = (xhat1 * cols_s[0, :, 0:1] + cols_s[1, :, 0:1]).astype(BF)
        tg_a[0:SPACE, :] += dot(n1_s[...].T, d_pre)
        dn1 = dot(d_pre, tw1t[...])[:, 0:patches]
        ln1_a[:, 0:1] += jnp.sum(dn1 * xhat1, axis=1, keepdims=True)
        ln1_a[:, 1:2] += jnp.sum(dn1, axis=1, keepdims=True)
        dxh = dn1 * cols_s[0, :, 0:1]
        first = jnp.sum(dxh, axis=0, keepdims=True) / width
        second = jnp.sum(dxh * xhat1, axis=0, keepdims=True) / width
        x_in[b] = (d_mid + rstd1 * (dxh - first - xhat1 * second)).astype(BF)
        for k in range(1, n_mp):
            grad_copy(k, b).start()
        own_grad(b).start()
        for k in range(images):
            if table["image", k]:
                pl.when(b == k)(functools.partial(slot_steps, table["image", k]))
        return 0

    def wait_tokens(b, _):
        for k in range(1, n_mp):
            token_copy(k, b).wait_send()
        return 0

    lax.fori_loop(0, images, wait_tokens, 0)

    for h in range(2):
        if h == 1:
            wide_load(1, 1).wait()
            dn_a[...] = dot_nt(wide_s[:, 0:deep], w1_s[...])
            wide_load(0, 0).start()
            slot_steps(table["dense",])
        lax.fori_loop(h * images // 2, (h + 1) * images // 2, token_backward, 0)

    group = groups[0]
    mine = member(group)
    t_half = t_b.shape[0] // 2
    s_rows = t_s2.shape[0]
    w_v = t_b.shape[1]
    va[0:2, :] = ln1_a[...].T[0:2, :]
    for row in range(7):
        for c in range(width // w_v):
            at = ROW + row * 2 + c
            tg_a[at : at + 1, :] = va[row : row + 1, c * w_v : (c + 1) * w_v]
    for c in range(0, deep, 128):
        at, col = ROW + 14 + c // w_v, c % w_v
        tg_a[at : at + 1, col : col + 128] = cb1_a[c // BLOCK, 0:1, c % BLOCK : c % BLOCK + 128]
    t_b[...] = tg_a[...].astype(BF)

    def spot(i):
        return pl.ds(pl.multiple_of(i * s_rows, 16), s_rows)

    def side(i):
        return pl.ds(pl.multiple_of(i * t_half, 16), t_half)

    sem = 0
    core_sum = remote(t_b.at[side(1 - core_bit)], t_r1, sm_s.at[0], sm_r.at[0], partner(core))
    sem += 1
    spread, back = [], []
    for g, team in enumerate(groups):
        copies = []
        for k in range(1, team[1] * team[2]):
            other, to = peer(team, k)
            src = t_r1.at[spot(other)] if g == 0 else t_s2
            copies.append(remote(src, t_r2.at[g, member(team)], sm_s.at[sem], sm_r.at[sem], to))
            sem += 1
        spread.append(copies)
    for k in range(1, group[1] * group[2]):
        _, to = peer(group, k)
        back.append(remote(t_s2, t_g.at[spot(mine)], sm_s.at[sem], sm_r.at[sem], to))
        sem += 1
    t_here = smt_o.at[side(core_bit)]
    core_back = remote(t_g, t_here, sm_s.at[sem], sm_r.at[sem], partner(core))
    own_small = pltpu.make_async_copy(t_g, t_here, sm_l.at[0])

    def sum_team(g):
        count = groups[g][1] * groups[g][2]
        acc = t_r2[g, 0].astype(F32)
        for k in range(1, count):
            acc = acc + t_r2[g, k].astype(F32)
        t_s2[...] = acc.astype(BF)

    core_sum.start()

    def out_rows(h):
        wide_load(0, h).wait()
        result = dot(wide_s[:, 0:deep], w2_s[...])
        for i in range(images // 2):
            b = h * images // 2 + i
            rows = result[i * patches : (i + 1) * patches, :]
            mid_p[b] = (mid_p[b].astype(F32) + rows + rows_s[4:5, :]).astype(BF)
        if h == 0:
            wide_load(0, 1).start()
        slot_steps(table["out", h])

    out_rows(0)
    core_sum.wait()
    t_r1[...] = (t_r1[...].astype(F32) + t_b[side(core_bit), :].astype(F32)).astype(BF)
    start(spread[0])
    t_r2[0, mine] = t_r1[spot(mine), :]
    out_rows(1)
    wait(spread[0])
    sum_team(0)
    for g in range(1, len(groups)):
        start(spread[g])
        t_r2[g, member(groups[g])] = t_s2[...]
        wait(spread[g])
        sum_team(g)
    start(back)
    t_g[spot(mine), :] = t_s2[...]

    for c in range(0, width, 128):
        cols = slice(c, c + 128)
        for b in range(images):
            mix_s[pl.ds(b, patches, stride=images), :] = mid_p[b, :, cols].astype(F32)
        n2_f[:, cols] = mix_s[...].astype(BF)
    own_out = pltpu.make_async_copy(n2_f, out_o, o_l.at[0])
    own_out.start()
    slot_steps(table["end",])
    wait(back)
    core_back.start()
    own_small.start()
    slot_steps(rest_steps)
    core_back.wait()
    own_small.wait()

    def wait_grads(b, _):
        for k in range(1, n_mp):
            other, to = mp_peer(k)
            grad_copy(k, b).wait_send()
            remote(
                x_in.at[b, channels(other)],
                dtok_o.at[other * images + b],
                out_s.at[k - 1, b],
                out_r.at[other, b],
                to,
            ).wait_recv()
        own_grad(b).wait()
        return 0

    lax.fori_loop(0, images, wait_grads, 0)
    own_out.wait()


def finish_kernel(
    out,
    dtok,
    gw,
    smt,
    out_o,
    dtok_o,
    g_ln1,
    b_ln1,
    g_tw1,
    g_tb1,
    g_tw2,
    g_tb2,
    g_ln2,
    b_ln2,
    g_cw1,
    g_cb1,
    g_cw2,
    g_cb2,
):
    @pl.when(pl.program_id(0) == 0)
    def _():
        patches, width = g_tw1.shape[0], g_ln1.shape[0]
        g_tw1[...] = smt[0:patches, :].astype(F32)
        g_tw2[...] = smt[SPACE : SPACE + patches, :].astype(F32)
        per = width // smt.shape[1]
        small = smt[ROW:SPACE, :].astype(F32)
        for row, ref in ((0, g_ln1), (1, b_ln1), (2, g_ln2), (3, b_ln2), (4, g_cb2), (5, g_tb1), (6, g_tb2), (7, g_cb1)):
            n = ref.shape[0]
            rows = [small[row * per + i : row * per + i + 1, :] for i in range(-(-n // smt.shape[1]))]
            ref[...] = jnp.concatenate(rows, axis=1)[:, 0:n].reshape(n)

    g_cw1[...] = gw[0].astype(F32)
    g_cw2[...] = gw[1].astype(F32).T
    out_o[...] = out[...]
    dtok_o[...] = dtok[...]


def body(tokens, cot, g1, c1, tw1, tb1, tw2, tb2, g2, c2, w1, b1, w2, b2):
    n_mp, n_dp = lax.axis_size("mp"), lax.axis_size("dp")
    images, patches, width = cot.shape
    hidden = tw1.shape[1]
    local = tokens.shape[2]
    deep = w1.shape[1]
    tokens = tokens.transpose(0, 2, 1)
    cot = cot.transpose(1, 0, 2).reshape(patches * images, width)
    tw2 = tw2.T
    blocks = deep // BLOCK
    streams = reduce_plan(n_mp, n_dp, width)
    groups = small_groups(n_mp, n_dp)
    total = images * patches
    stage_rows = [have for _, _, stages in streams for _, have, _ in stages]
    n_ids = 1 + len(stage_rows)
    team = groups[0][1] * groups[0][2]
    n_small = 2 + team - 1 + sum(size * across - 1 for _, size, across in groups)
    s_rows = SPACE // team
    hbm, vmem = pl.BlockSpec(memory_space=pl.ANY), pl.BlockSpec(memory_space=pltpu.VMEM)
    dma = pltpu.SemaphoreType.DMA
    scratch = [
        pltpu.VMEM((images, width, patches), BF),
        pltpu.VMEM((patches, width), BF),
        pltpu.VMEM((images, patches, width), BF),
        pltpu.VMEM((total, width), BF),
        pltpu.VMEM((total, width), BF),
        pltpu.VMEM((total // 2, max(deep, 2 * (-(-total // 128) * 128))), BF),
        pltpu.VMEM((2, 2, width, hidden), BF),
        pltpu.VMEM((total // 2, width), F32),
        pltpu.VMEM((patches, width), F32),
        pltpu.VMEM((total, 128), F32),
        pltpu.VMEM((2, 2, total, BLOCK), BF),
        pltpu.VMEM((width, deep), BF),
        pltpu.VMEM((deep, width), BF),
        pltpu.VMEM((2, width, BLOCK), BF),
        pltpu.VMEM((blocks, width, BLOCK), BF),
        [pltpu.VMEM((blocks, rows, BLOCK), BF) for rows in stage_rows],
        pltpu.VMEM((width, SPACE), BF),
        pltpu.VMEM((SPACE, width), BF),
        pltpu.VMEM((width, SPACE), BF),
        pltpu.VMEM((SPACE, hidden), BF),
        pltpu.VMEM((hidden, SPACE), BF),
        pltpu.VMEM((hidden, SPACE), BF),
        pltpu.VMEM((SPACE, hidden), BF),
        pltpu.VMEM((8, width), F32),
        pltpu.VMEM((blocks, 8, BLOCK), F32),
        pltpu.VMEM((2, width, 128), F32),
        pltpu.VMEM((blocks, 8, BLOCK), F32),
        pltpu.VMEM((8, width), F32),
        pltpu.VMEM((width, 128), F32),
        pltpu.VMEM((2 * SPACE, hidden), F32),
        pltpu.VMEM((2 * SPACE, hidden), BF),
        pltpu.VMEM((SPACE, hidden), BF),
        pltpu.VMEM((len(groups), team, s_rows, hidden), BF),
        pltpu.VMEM((s_rows, hidden), BF),
        pltpu.VMEM((SPACE, hidden), BF),
        dma((n_mp - 1, images)),
        dma((n_mp, images)),
        dma((images,)),
        dma((1,)),
        dma((2,)),
        dma((1,)),
        dma((2, 2)),
        dma((2, 2, 2, 2)),
        dma((2, 2)),
        dma((n_mp - 1, images)),
        dma((n_mp, images)),
        dma((images,)),
        dma((n_ids, blocks)),
        dma((n_ids, blocks)),
        dma((n_ids + len(streams), blocks)),
        dma((n_ids + len(streams), blocks)),
        dma((len(streams), blocks)),
        dma((n_small,)),
        dma((n_small,)),
        dma((1,)),
    ]
    out, dtok, gw, smt, _, _ = pl.pallas_call(
        functools.partial(layer_kernel, n_mp, n_dp, streams, groups),
        out_shape=(
            jax.ShapeDtypeStruct(cot.shape, BF),
            jax.ShapeDtypeStruct(tokens.shape, BF),
            jax.ShapeDtypeStruct((2, width, deep), BF),
            jax.ShapeDtypeStruct((2 * SPACE, hidden), BF),
            jax.ShapeDtypeStruct((images, 2, width, hidden), BF),
            jax.ShapeDtypeStruct((2, total, deep), BF),
        ),
        in_specs=[hbm] * 4 + [vmem] * 10,
        out_specs=(hbm,) * 6,
        scratch_shapes=scratch,
        compiler_params=pltpu.CompilerParams(
            collective_id=0, has_side_effects=True, vmem_limit_bytes=VMEM_LIMIT
        ),
    )(tokens, cot, w1, w2, g1, c1, tw1, tb1, tw2, tb2, g2, c2, b1, b2)
    full = lambda n: jax.ShapeDtypeStruct((n,), F32)
    out_spec = pl.BlockSpec((total, width // blocks), lambda j: (0, j // 2))
    dtok_spec = pl.BlockSpec((n_mp * images // 2, local // blocks, patches), lambda j: (j % 2, j // 2, 0))
    results = pl.pallas_call(
        finish_kernel,
        grid=(2 * blocks,),
        out_shape=(
            jax.ShapeDtypeStruct(out.shape, BF),
            jax.ShapeDtypeStruct(dtok.shape, BF),
            full(width),
            full(width),
            jax.ShapeDtypeStruct((patches, hidden), F32),
            full(hidden),
            jax.ShapeDtypeStruct((patches, hidden), F32),
            full(patches),
            full(width),
            full(width),
            jax.ShapeDtypeStruct((width, deep), F32),
            full(deep),
            jax.ShapeDtypeStruct((deep, width), F32),
            full(width),
        ),
        in_specs=[out_spec, dtok_spec, pl.BlockSpec((2, width, BLOCK // 2), lambda j: (0, 0, j)), vmem],
        out_specs=(
            (out_spec, dtok_spec)
            + (vmem,) * 8
            + (
                pl.BlockSpec((width, BLOCK // 2), lambda j: (0, j)),
                vmem,
                pl.BlockSpec((BLOCK // 2, width), lambda j: (j, 0)),
                vmem,
            )
        ),
        compiler_params=pltpu.CompilerParams(vmem_limit_bytes=VMEM_LIMIT),
    )(out, dtok, gw, smt)
    out, dtok, *grads = results
    grads[4] = grads[4].T
    return (out.reshape(patches, images, width).transpose(1, 0, 2), dtok.transpose(0, 2, 1), *grads)


def solution(mesh):
    placed = (P("dp", None, "mp"), P(("dp", "mp"), None, None)) + (P(),) * 12
    return jax.shard_map(body, mesh=mesh, in_specs=placed, out_specs=(placed[1], placed[0]) + (P(),) * 12, check_vma=False)
```

```python
import functools

import jax
import jax.numpy as jnp
from jax import lax
from jax.experimental import pallas as pl
from jax.experimental.pallas import tpu as pltpu
from jax.sharding import PartitionSpec as P

BF = jnp.bfloat16
F32 = jnp.float32
EPS = 1e-06
MESH = pl.DeviceIdType.MESH
NT = (((1,), (1,)), ((), ()))

BLOCK = 512
ROW = 200
VMEM_LIMIT = 64 * 2**20 - 2**16
SPACE = 256
PLAN = (
    (),
    (),
    (10000,),
    (),
    (10100,),
    (20000, 30000, 40000),
    (10200,),
    (30001, 20100, 30100, 40100, 20001),
    (10300, 40001),
    (20002, 30002, 20101, 30101, 20200, 40101, 30200, 40200),
    (10400, 40002, 20300, 30300, 40300),
    (20003, 30003, 20102, 30102, 40102, 20201, 30201, 40201),
    (10500, 40003),
    (20303, 30303, 40303, 20402, 30402, 40402, 30501, 40005, 20006, 40105, 20204, 30204, 20502, 40204, 30105, 20105, 40502),
    (40103, 20301, 30301, 40301, 30202, 20400, 30400, 40400, 20004),
    (20103, 30103, 20202, 40202, 20500, 30500, 30004, 40004, 40104, 40500),
    (30203, 20302, 30302, 40302, 20401, 30401, 40401, 20005),
    (20203, 40203, 20501, 40501, 30005, 20104, 30104),
    (30006,),
    (40403, 20403, 30403, 30502, 40503, 40006, 20503, 30205, 40106, 20205, 20304, 20106, 40205, 30304, 30106, 40304),
    (20007, 30007),
    (30503, 20404, 30404, 40404, 20504, 40504),
    (20008, 30008, 30107, 20206, 30206, 40206, 20305, 30305, 40305),
    (40007, 20107, 40107, 30108, 20405, 30405, 40405, 30504, 20505, 40505),
    (40207, 20306, 30306, 40306),
    (40008, 20108, 40108, 20207, 30207, 40208, 30406, 30505, 20208, 30208, 20406, 40406, 20307, 20506, 40506, 20308, 30506, 40307, 40308, 20407, 20408, 30307, 20507, 30407, 40407, 40507, 30507, 30308, 30408, 20508, 40408, 40508, 30508),
)


def dot(a, b):
    return jnp.dot(a, b, preferred_element_type=F32)


def dot_nt(a, b):
    return lax.dot_general(a, b, NT, preferred_element_type=F32)


def gelu_both(v):
    cdf = 0.5 + 0.5 * lax.erf(v * 0.7071067811865476)
    return v * cdf, cdf + v * (jnp.exp(-0.5 * v * v) * 0.3989422804014327)


def standardize(v, axis):
    width = v.shape[axis]
    mean = jnp.sum(v, axis=axis, keepdims=True) / width
    square = jnp.sum(v * v, axis=axis, keepdims=True) / width
    rstd = lax.rsqrt(square - mean * mean + EPS)
    return (v - mean) * rstd, rstd


def bits_of(n):
    return n.bit_length() - 1


def reduce_plan(n_mp, n_dp, width):
    dp = [("dp", b) for b in range(bits_of(n_dp))]
    mp = [("mp", b) for b in range(1, bits_of(n_mp))]
    if len(dp) == 3 and len(mp) == 1:
        third = width // 3
        orders = ([mp[0], dp[0], dp[1], dp[2]], [dp[0], dp[1], mp[0], dp[2]], [dp[1], dp[0], dp[2], mp[0]])
        raw = [(s * third, third, order) for s, order in enumerate(orders)]
    else:
        raw = [(0, width, dp + mp)]
    streams = []
    for base, rows, keys in raw:
        stages, have = [], rows
        for key in keys:
            halved = have % 32 == 0
            have = have // 2 if halved else have
            stages.append((key, have, halved))
        streams.append((base, rows, stages))
    return streams


def small_groups(n_mp, n_dp):
    size = min(8, n_dp)
    groups, stride = [(1, size, n_mp // 2)], size
    while stride < n_dp:
        size = min(8, n_dp // stride)
        groups.append((stride, size, 1))
        stride *= size
    return groups


def plan_steps(blocks, images, streams):
    pieces = [("block", j, p) for j in range(blocks) for p in range(2)] + [("loop",), ("dense",)]
    pieces += [("image", b) for b in range(images)] + [("out", h) for h in range(2)] + [("end",)]
    if len(streams) == 3 and len(PLAN) == len(pieces) + 1:
        return dict(zip(pieces, PLAN)), PLAN[-1]
    table = {piece: [] for piece in pieces}
    for j in range(blocks):
        table[("block", j + 1, 0) if j + 1 < blocks else ("loop",)].append(10000 + 100 * j)
    last = max(len(stages) + sum(halved for _, _, halved in stages) for _, _, stages in streams)
    return table, [20000 + 10000 * s + 100 * j + k for k in range(last + 1) for j in range(blocks) for s in range(len(streams))]


def layer_kernel(
    n_mp,
    n_dp,
    streams,
    groups,
    tokens,
    cot,
    w1,
    w2,
    g1,
    c1,
    tw1,
    tb1,
    tw2,
    tb2,
    g2,
    c2,
    b1,
    b2,
    out_o,
    dtok_o,
    gw_o,
    smt_o,
    tok_h,
    hid_h,
    x_in,
    g_in,
    mid_p,
    g_f,
    n2_f,
    wide_s,
    tok_s,
    dn_a,
    dm_a,
    mix_s,
    hid_s,
    w1_s,
    w2_s,
    part,
    r0,
    rest,
    n1_s,
    dm_s,
    dm_t,
    tw1p,
    tw1t,
    tw2p,
    tw2t,
    rows_s,
    b1_s,
    cols_s,
    cb1_a,
    va,
    ln1_a,
    tg_a,
    t_b,
    t_r1,
    t_r2,
    t_s2,
    t_g,
    in_s,
    in_r,
    in_l,
    g_l,
    w_l,
    o_l,
    tok_l,
    hid_l,
    wide_l,
    out_s,
    out_r,
    out_l,
    rs_s,
    rs_r,
    ag_s,
    ag_r,
    own_l,
    sm_s,
    sm_r,
    sm_l,
):
    images, width, patches = x_in.shape
    local = tokens.shape[1]
    hidden = tw1.shape[1]
    blocks = w1.shape[1] // BLOCK
    total = images * patches
    half = total // 2
    mp_me = lax.axis_index("mp")
    dp_me = lax.axis_index("dp")

    bits, partners = {}, {}
    for key in [("mp", b) for b in range(bits_of(n_mp))] + [("dp", b) for b in range(bits_of(n_dp))]:
        axis, b = key
        me = mp_me if axis == "mp" else dp_me
        bits[key] = lax.rem(lax.div(me, 1 << b), 2)
        partners[key] = {axis: me + (1 << b) * (1 - 2 * bits[key])}
    bit_of, partner = bits.__getitem__, partners.__getitem__

    members, peers = {}, {}
    for group in groups:
        stride, size, across = group
        index = lax.rem(lax.div(dp_me, stride), size)
        members[group] = index * across + lax.div(mp_me, 2) if across > 1 else index
        peers[group] = []
        for k in range(1, size * across):
            other = lax.rem(members[group] + k, size * across)
            to = {"dp": dp_me + (lax.div(other, across) - index) * stride}
            if across > 1:
                to["mp"] = lax.rem(other, across) * 2 + lax.rem(mp_me, 2)
            peers[group].append((other, to))
    member = members.__getitem__

    def peer(group, k):
        return peers[group][k - 1]

    mp_peers = [lax.rem(mp_me + k, n_mp) for k in range(n_mp)]

    def mp_peer(k):
        return mp_peers[k], {"mp": mp_peers[k]}

    def remote(src, dst, send, recv, to):
        return pltpu.make_async_remote_copy(
            src_ref=src, dst_ref=dst, send_sem=send, recv_sem=recv, device_id=to, device_id_type=MESH
        )

    barrier = pltpu.get_barrier_semaphore()
    greet = [peer(group, k)[1] for group in groups for k in range(1, group[1] * group[2])]
    greet += [{"mp": (mp_me // 2 + k) % (n_mp // 2) * 2 + 1 - mp_me % 2} for k in range(n_mp // 2)]
    for to in greet:
        pl.semaphore_signal(barrier, inc=1, device_id=to, device_id_type=MESH)

    def channels(member):
        return pl.ds(pl.multiple_of(member * local, 16), local)

    def own_tokens(b):
        return pltpu.make_async_copy(tokens.at[mp_me * images + b], x_in.at[b, channels(mp_me)], in_l.at[b])

    own_cot = pltpu.make_async_copy(cot, n2_f, g_l.at[0])

    weights = (
        pltpu.make_async_copy(w1, w1_s, w_l.at[0]),
        pltpu.make_async_copy(w2, w2_s, w_l.at[1]),
    )

    def load_own(b, _):
        own_tokens(b).start()
        return 0

    own_cot.start()
    lax.fori_loop(0, images, load_own, 0)
    pl.semaphore_wait(barrier, len(greet))

    def token_copy(k, b):
        other, to = mp_peer(k)
        return remote(
            tokens.at[other * images + b], x_in.at[b, channels(mp_me)], in_s.at[k - 1, b], in_r.at[mp_me, b], to
        )

    def send_tokens(b, _):
        for k in range(1, n_mp):
            token_copy(k, b).start()
        return 0

    lax.fori_loop(0, images, send_tokens, 0)
    for copy in weights:
        copy.start()

    for row, ref in ((0, g1), (1, c1), (2, g2), (3, c2), (4, b2)):
        rows_s[row : row + 1, :] = ref[...].reshape(1, width)
    for j in range(blocks):
        b1_s[j, 0:1, :] = b1[j * BLOCK : (j + 1) * BLOCK].reshape(1, BLOCK)
    rows_s[5:6, 0:hidden] = tb1[...].reshape(1, hidden)
    rows_s[6:7, 0:patches] = tb2[...].reshape(1, patches)
    cols_s[0] = jnp.broadcast_to(rows_s[0:1, :], (128, width)).T
    cols_s[1] = jnp.broadcast_to(rows_s[1:2, :], (128, width)).T
    tw1p[...] = jnp.zeros_like(tw1p)
    tw1p[0:patches, :] = tw1[...]
    tw1t[...] = tw1p[...].T
    tw2t[...] = jnp.zeros_like(tw2t)
    tw2t[0:patches, :] = tw2[...]
    tw2p[...] = tw2t[...].T
    n1_s[...] = jnp.zeros_like(n1_s)
    dm_s[...] = jnp.zeros_like(dm_s)
    va[...] = jnp.zeros_like(va)
    ln1_a[...] = jnp.zeros_like(ln1_a)
    dm_t[...] = jnp.zeros_like(dm_t)
    tg_a[...] = jnp.zeros_like(tg_a)
    cb1_a[...] = jnp.zeros_like(cb1_a)

    own_cot.wait()
    for c in range(0, width, 128):
        cols = slice(c, c + 128)
        wide = n2_f[:, cols].astype(F32)
        va[4:5, cols] = jnp.sum(wide, axis=0, keepdims=True)
        mix_s[...] = wide
        for b in range(images):
            g_f[b * patches : (b + 1) * patches, cols] = mix_s[pl.ds(b, patches, stride=images), :].astype(BF)

    aside = -(-total // 128) * 128

    def transpose_rows(src, at, first=0, last=total):
        for lo in range(first, last, 128):
            hi = min(lo + 128, total)
            wide_s[0:width, at + lo : at + hi] = src[lo:hi, :].T

    transpose_rows(g_f, aside)

    def token_save(b):
        return pltpu.make_async_copy(tok_s.at[lax.rem(b, 2)], tok_h.at[b], tok_l.at[0, lax.rem(b, 2)])

    def token_load(b):
        return pltpu.make_async_copy(tok_h.at[b], tok_s.at[lax.rem(b, 2)], tok_l.at[1, lax.rem(b, 2)])

    def token_forward(b, _):
        for k in range(1, n_mp):
            other, to = mp_peer(k)
            remote(
                tokens.at[mp_me * images + b],
                x_in.at[b, channels(other)],
                in_s.at[k - 1, b],
                in_r.at[other, b],
                to,
            ).wait_recv()
        own_tokens(b).wait()
        x = x_in[b].astype(F32)
        xhat, _ = standardize(x, 0)
        n1_s[:, 0:patches] = (xhat * cols_s[0, :, 0:1] + cols_s[1, :, 0:1]).astype(BF)
        act, slope = gelu_both(dot(n1_s[...], tw1p[...]) + rows_s[5:6, 0:hidden])
        act = act.astype(BF)

        @pl.when(b >= 2)
        def _():
            token_save(b - 2).wait()

        slot = lax.rem(b, 2)
        tok_s[slot, 0] = act
        tok_s[slot, 1] = slope.astype(BF)
        token_save(b).start()
        mixed = dot(act, tw2p[...])[:, 0:patches] + rows_s[6:7, 0:patches]
        dm_t[:, 0:patches] = (x + mixed).astype(BF)
        mid_p[b] = dm_t[...].T[0:patches, :]
        return 0

    def second_norm(first, last):
        for b in range(first, last):
            xhat, _ = standardize(mid_p[b].astype(F32), 1)
            n2_f[b * patches : (b + 1) * patches, :] = (xhat * rows_s[2:3, :] + rows_s[3:4, :]).astype(BF)

    def unit(h, j):
        slot = lax.rem(j, 2)
        rows = slice(h * half, (h + 1) * half)
        for lo in range(0, BLOCK, 256):
            here = pl.ds(pl.multiple_of(j * BLOCK + lo, 256), 256)
            cols = slice(lo, lo + 256)
            act, slope = gelu_both(dot(n2_f[rows, :], w1_s[:, here]) + b1_s[j, 0:1, cols])
            hid_s[slot, 0, rows, cols] = act.astype(BF)
            dp = dot_nt(g_f[rows, :], w2_s[here, :]) * slope
            cb1_a[j, 0:1, cols] += jnp.sum(dp, axis=0, keepdims=True)
            hid_s[slot, 1, rows, cols] = dp.astype(BF)

    def hidden_copies(kind, h, j):
        slot = lax.rem(j, 2)
        rows = pl.ds(h * half, half)
        cols = pl.ds(pl.multiple_of(j * BLOCK, BLOCK), BLOCK)
        pairs = [(hid_s.at[slot, i, rows, :], hid_h.at[i, rows, cols]) for i in range(2)]
        return [
            pltpu.make_async_copy(here if kind == 0 else there, there if kind == 0 else here, hid_l.at[kind, h, i, slot])
            for i, (here, there) in enumerate(pairs)
        ]

    def start(copies):
        for copy in copies:
            copy.start()

    def wait(copies):
        for copy in copies:
            copy.wait()

    lax.fori_loop(0, images // 2, token_forward, 0)
    second_norm(0, images // 2)
    wait(weights)

    def early(j, _):
        @pl.when(j >= 2)
        def _():
            wait(hidden_copies(0, 0, j - 2))

        unit(0, j)
        start(hidden_copies(0, 0, j))
        cols = pl.ds(pl.multiple_of(j * BLOCK, BLOCK), BLOCK)
        dn_a[...] += dot_nt(hid_s[lax.rem(j, 2), 1, 0:half, :], w1_s[:, cols])

        @pl.when((j % 2 == 1) & (j < images - 4))
        def _():
            token_forward(images // 2 + j // 2, 0)

        return 0

    dn_a[...] = jnp.zeros_like(dn_a)
    lax.fori_loop(0, blocks, early, 0)
    for j in range(blocks - 2, blocks):
        wait(hidden_copies(0, 0, j))
    start(hidden_copies(1, 0, 0))
    lax.fori_loop(images - 2, images - 1, token_forward, 0)
    second_norm(images // 2, images - 1)
    ahead = (images - 1) * patches // 128 * 128
    transpose_rows(n2_f, 0, 0, ahead)
    lax.fori_loop(images - 1, images, token_forward, 0)
    for b in range(images - 2, images):
        token_save(b).wait()
    second_norm(images - 1, images)
    transpose_rows(n2_f, 0, ahead)

    core = ("mp", 0)
    core_bit = bit_of(core)

    ids = {}
    for s, (_, _, stages) in enumerate(streams):
        for t in range(len(stages)):
            ids[s, t] = 1 + len(ids)
    held = []
    for base, rows, stages in streams:
        line, off = [(base, rows)], base
        for key, have, halved in stages:
            off = off + bit_of(key) * have if halved else off
            line.append((off, have))
        held.append(line)

    def region(s, t):
        off, rows = held[s][t]
        return pl.ds(off if isinstance(off, int) else pl.multiple_of(off, 16), rows)

    def sums(s, t, j):
        return rest[ids[s, t] - 1].at[j]

    def source(s, t, j):
        base, _, _ = streams[s]
        return (r0.at[j], base) if t == 0 else (sums(s, t - 1, j), 0)

    def core_copy(j):
        return remote(part.at[1 - core_bit], r0.at[j], rs_s.at[0, j], rs_r.at[0, j], partner(core))

    def stage_copy(s, t, j):
        key, rows, halved = streams[s][2][t]
        ref, low = source(s, t, j)
        low = low + (1 - bit_of(key)) * rows if halved else low
        if not isinstance(low, int):
            low = pl.multiple_of(low, 16)
        i = ids[s, t]
        return remote(ref.at[pl.ds(low, rows)], sums(s, t, j), rs_s.at[i, j], rs_r.at[i, j], partner(key))

    def add_rows(dst, src, low, rows, into=None, at=0):
        chunk = next(c for c in (64, 48, 32, 16) if rows % c == 0)

        def step(i, _):
            here = pl.ds(pl.multiple_of(i * chunk, 16), chunk)
            there = pl.ds(pl.multiple_of(low + i * chunk, 16), chunk)
            result = dst[here, :] + src[there, :]
            if into is None:
                dst[here, :] = result
            else:
                into[pl.ds(pl.multiple_of(at + i * chunk, 16), chunk), :] = result
            return 0

        lax.fori_loop(0, rows // chunk, step, 0)

    def finish_core(j):
        core_copy(j).wait()
        add_rows(r0.at[j], part.at[core_bit], 0, width)

    def finish_stage(s, t, j):
        stage_copy(s, t, j).wait()
        key, rows, halved = streams[s][2][t]
        ref, low = source(s, t, j)
        low = low + bit_of(key) * rows if halved else low
        if t == n_rs - 1:
            add_rows(sums(s, t, j), ref, low, rows, r0.at[j], held[s][n_rs][0])
        else:
            add_rows(sums(s, t, j), ref, low, rows)

    gathers = [[t for t in reversed(range(len(stages))) if stages[t][2]] for _, _, stages in streams]

    def own_copy(s, j):
        base, rows, _ = streams[s]
        there = gw_o.at[core_bit, pl.ds(base, rows), pl.ds(j * BLOCK, BLOCK)]
        return pltpu.make_async_copy(r0.at[j, pl.ds(base, rows), :], there, own_l.at[s, j])

    def gather_copy(s, a, j):
        t = gathers[s][a]
        key = streams[s][2][t][0]
        here = r0.at[j, region(s, t + 1), :]
        i = ids[s, t]
        return remote(here, here, ag_s.at[i, j], ag_r.at[i, j], partner(key))

    def gather_core(s, j):
        base, rows, _ = streams[s]
        there = gw_o.at[core_bit, pl.ds(base, rows), pl.ds(j * BLOCK, BLOCK)]
        i = 1 + len(ids) + s
        return remote(r0.at[j, pl.ds(base, rows), :], there, ag_s.at[i, j], ag_r.at[i, j], partner(core))

    n_rs = len(streams[0][2])
    every = range(len(streams))

    def advance(item):
        s, j, k = item // 10000 - 2, item // 100 % 100, item % 100
        if s < 0:
            finish_core(j)
            for s in every:
                stage_copy(s, 0, j).start()
            return
        n_ag = len(gathers[s])
        if k < n_rs:
            finish_stage(s, k, j)
        elif k < n_rs + n_ag:
            gather_copy(s, k - n_rs, j).wait()
        else:
            gather_core(s, j).wait()
            own_copy(s, j).wait()
        k += 1
        if k < n_rs:
            stage_copy(s, k, j).start()
        elif k < n_rs + n_ag:
            gather_copy(s, k - n_rs, j).start()
        elif k == n_rs + n_ag:
            gather_core(s, j).start()
            own_copy(s, j).start()

    table, rest_steps = plan_steps(blocks, images, streams)

    def slot_steps(items):
        for item in items:
            advance(item)

    def block_step(j, _):
        wait(hidden_copies(1, 0, j))

        @pl.when(j >= 2)
        def _():
            wait(hidden_copies(0, 1, j - 2))

        unit(1, j)
        start(hidden_copies(0, 1, j))

        @pl.when(j + 1 < blocks)
        def _():
            start(hidden_copies(1, 0, j + 1))

        for k in range(blocks):
            if table["block", k, 0]:
                pl.when(j == k)(functools.partial(slot_steps, table["block", k, 0]))
        slot = lax.rem(j, 2)
        part[0] = dot(wide_s[0:width, 0:total], hid_s[slot, 1]).astype(BF)
        part[1] = dot(wide_s[0:width, aside : aside + total], hid_s[slot, 0]).astype(BF)
        core_copy(j).start()
        for k in range(blocks):
            if table["block", k, 1]:
                pl.when(j == k)(functools.partial(slot_steps, table["block", k, 1]))
        return 0

    lax.fori_loop(0, blocks, block_step, 0)
    slot_steps(table["loop",])
    for j in range(blocks - 2, blocks):
        wait(hidden_copies(0, 1, j))

    deep = blocks * BLOCK

    def wide_load(i, h):
        return pltpu.make_async_copy(hid_h.at[i, pl.ds(h * half, half)], wide_s.at[:, pl.ds(0, deep)], wide_l.at[i, h])

    wide_load(1, 1).start()
    token_load(0).start()

    def grad_copy(k, b):
        other, to = mp_peer(k)
        return remote(
            x_in.at[b, channels(other)], dtok_o.at[mp_me * images + b], out_s.at[k - 1, b], out_r.at[mp_me, b], to
        )

    def own_grad(b):
        return pltpu.make_async_copy(x_in.at[b, channels(mp_me)], dtok_o.at[mp_me * images + b], out_l.at[b])

    def token_backward(b, _):
        q = lax.rem(b, images // 2)

        @pl.when(b + 1 < images)
        def _():
            token_load(b + 1).start()

        xhat2, rstd2 = standardize(mid_p[b].astype(F32), 1)
        for i in range(images // 2):

            @pl.when(q == i)
            def _():
                quad = g_f.at[pl.ds(pl.multiple_of(half * (b // (images // 2)), 16), half)]
                g_in[...] = quad[i * patches : (i + 1) * patches, :]
                dm_a[...] = dn_a[i * patches : (i + 1) * patches, :]

        dn2 = dm_a[...]
        va[2:3, :] += jnp.sum(dn2 * xhat2, axis=0, keepdims=True)
        va[3:4, :] += jnp.sum(dn2, axis=0, keepdims=True)
        dxh = dn2 * rows_s[2:3, :]
        first = jnp.sum(dxh, axis=-1, keepdims=True) / width
        second = jnp.sum(dxh * xhat2, axis=-1, keepdims=True) / width
        dm_s[0:patches, :] = (g_in[...].astype(F32) + rstd2 * (dxh - first - xhat2 * second)).astype(BF)
        dm_t[...] = dm_s[...].T
        d_mid = dm_t[:, 0:patches].astype(F32)
        va[6:7, 0:patches] += jnp.sum(d_mid, axis=0, keepdims=True)
        token_load(b).wait()
        slot = lax.rem(b, 2)
        d_pre = dot(dm_t[...], tw2t[...]) * tok_s[slot, 1].astype(F32)
        va[5:6, 0:hidden] += jnp.sum(d_pre, axis=0, keepdims=True)
        d_pre = d_pre.astype(BF)
        tg_a[SPACE:, :] += dot(dm_s[...], tok_s[slot, 0])
        xhat1, rstd1 = standardize(x_in[b].astype(F32), 0)
        n1_s[:, 0:patches] = (xhat1 * cols_s[0, :, 0:1] + cols_s[1, :, 0:1]).astype(BF)
        tg_a[0:SPACE, :] += dot(n1_s[...].T, d_pre)
        dn1 = dot(d_pre, tw1t[...])[:, 0:patches]
        ln1_a[:, 0:1] += jnp.sum(dn1 * xhat1, axis=1, keepdims=True)
        ln1_a[:, 1:2] += jnp.sum(dn1, axis=1, keepdims=True)
        dxh = dn1 * cols_s[0, :, 0:1]
        first = jnp.sum(dxh, axis=0, keepdims=True) / width
        second = jnp.sum(dxh * xhat1, axis=0, keepdims=True) / width
        x_in[b] = (d_mid + rstd1 * (dxh - first - xhat1 * second)).astype(BF)
        for k in range(1, n_mp):
            grad_copy(k, b).start()
        own_grad(b).start()
        for k in range(images):
            if table["image", k]:
                pl.when(b == k)(functools.partial(slot_steps, table["image", k]))
        return 0

    def wait_tokens(b, _):
        for k in range(1, n_mp):
            token_copy(k, b).wait_send()
        return 0

    lax.fori_loop(0, images, wait_tokens, 0)

    for h in range(2):
        if h == 1:
            wide_load(1, 1).wait()
            dn_a[...] = dot_nt(wide_s[:, 0:deep], w1_s[...])
            wide_load(0, 0).start()
            slot_steps(table["dense",])
        lax.fori_loop(h * images // 2, (h + 1) * images // 2, token_backward, 0)

    group = groups[0]
    mine = member(group)
    t_half = t_b.shape[0] // 2
    s_rows = t_s2.shape[0]
    w_v = t_b.shape[1]
    va[0:2, :] = ln1_a[...].T[0:2, :]
    for row in range(7):
        for c in range(width // w_v):
            at = ROW + row * 2 + c
            tg_a[at : at + 1, :] = va[row : row + 1, c * w_v : (c + 1) * w_v]
    for c in range(0, deep, 128):
        at, col = ROW + 14 + c // w_v, c % w_v
        tg_a[at : at + 1, col : col + 128] = cb1_a[c // BLOCK, 0:1, c % BLOCK : c % BLOCK + 128]
    t_b[...] = tg_a[...].astype(BF)

    def spot(i):
        return pl.ds(pl.multiple_of(i * s_rows, 16), s_rows)

    def side(i):
        return pl.ds(pl.multiple_of(i * t_half, 16), t_half)

    sem = 0
    core_sum = remote(t_b.at[side(1 - core_bit)], t_r1, sm_s.at[0], sm_r.at[0], partner(core))
    sem += 1
    spread, back = [], []
    for g, team in enumerate(groups):
        copies = []
        for k in range(1, team[1] * team[2]):
            other, to = peer(team, k)
            src = t_r1.at[spot(other)] if g == 0 else t_s2
            copies.append(remote(src, t_r2.at[g, member(team)], sm_s.at[sem], sm_r.at[sem], to))
            sem += 1
        spread.append(copies)
    for k in range(1, group[1] * group[2]):
        _, to = peer(group, k)
        back.append(remote(t_s2, t_g.at[spot(mine)], sm_s.at[sem], sm_r.at[sem], to))
        sem += 1
    t_here = smt_o.at[side(core_bit)]
    core_back = remote(t_g, t_here, sm_s.at[sem], sm_r.at[sem], partner(core))
    own_small = pltpu.make_async_copy(t_g, t_here, sm_l.at[0])

    def sum_team(g):
        count = groups[g][1] * groups[g][2]
        acc = t_r2[g, 0].astype(F32)
        for k in range(1, count):
            acc = acc + t_r2[g, k].astype(F32)
        t_s2[...] = acc.astype(BF)

    core_sum.start()

    def out_rows(h):
        wide_load(0, h).wait()
        result = dot(wide_s[:, 0:deep], w2_s[...])
        for i in range(images // 2):
            b = h * images // 2 + i
            rows = result[i * patches : (i + 1) * patches, :]
            mid_p[b] = (mid_p[b].astype(F32) + rows + rows_s[4:5, :]).astype(BF)
        if h == 0:
            wide_load(0, 1).start()
        slot_steps(table["out", h])

    out_rows(0)
    core_sum.wait()
    t_r1[...] = (t_r1[...].astype(F32) + t_b[side(core_bit), :].astype(F32)).astype(BF)
    start(spread[0])
    t_r2[0, mine] = t_r1[spot(mine), :]
    out_rows(1)
    wait(spread[0])
    sum_team(0)
    for g in range(1, len(groups)):
        start(spread[g])
        t_r2[g, member(groups[g])] = t_s2[...]
        wait(spread[g])
        sum_team(g)
    start(back)
    t_g[spot(mine), :] = t_s2[...]

    for c in range(0, width, 128):
        cols = slice(c, c + 128)
        for b in range(images):
            mix_s[pl.ds(b, patches, stride=images), :] = mid_p[b, :, cols].astype(F32)
        n2_f[:, cols] = mix_s[...].astype(BF)
    own_out = pltpu.make_async_copy(n2_f, out_o, o_l.at[0])
    own_out.start()
    slot_steps(table["end",])
    wait(back)
    core_back.start()
    own_small.start()
    slot_steps(rest_steps)
    core_back.wait()
    own_small.wait()

    def wait_grads(b, _):
        for k in range(1, n_mp):
            other, to = mp_peer(k)
            grad_copy(k, b).wait_send()
            remote(
                x_in.at[b, channels(other)],
                dtok_o.at[other * images + b],
                out_s.at[k - 1, b],
                out_r.at[other, b],
                to,
            ).wait_recv()
        own_grad(b).wait()
        return 0

    lax.fori_loop(0, images, wait_grads, 0)
    own_out.wait()


def finish_kernel(
    out,
    dtok,
    gw,
    smt,
    out_o,
    dtok_o,
    g_ln1,
    b_ln1,
    g_tw1,
    g_tb1,
    g_tw2,
    g_tb2,
    g_ln2,
    b_ln2,
    g_cw1,
    g_cb1,
    g_cw2,
    g_cb2,
):
    @pl.when(pl.program_id(0) == 0)
    def _():
        patches, width = g_tw1.shape[0], g_ln1.shape[0]
        g_tw1[...] = smt[0:patches, :].astype(F32)
        g_tw2[...] = smt[SPACE : SPACE + patches, :].astype(F32)
        per = width // smt.shape[1]
        small = smt[ROW:SPACE, :].astype(F32)
        for row, ref in ((0, g_ln1), (1, b_ln1), (2, g_ln2), (3, b_ln2), (4, g_cb2), (5, g_tb1), (6, g_tb2), (7, g_cb1)):
            n = ref.shape[0]
            rows = [small[row * per + i : row * per + i + 1, :] for i in range(-(-n // smt.shape[1]))]
            ref[...] = jnp.concatenate(rows, axis=1)[:, 0:n].reshape(n)

    g_cw1[...] = gw[0].astype(F32)
    g_cw2[...] = gw[1].astype(F32).T
    out_o[...] = out[...]
    dtok_o[...] = dtok[...]


def body(tokens, cot, g1, c1, tw1, tb1, tw2, tb2, g2, c2, w1, b1, w2, b2):
    n_mp, n_dp = lax.axis_size("mp"), lax.axis_size("dp")
    images, patches, width = cot.shape
    hidden = tw1.shape[1]
    local = tokens.shape[2]
    deep = w1.shape[1]
    tokens = tokens.transpose(0, 2, 1)
    cot = cot.transpose(1, 0, 2).reshape(patches * images, width)
    tw2 = tw2.T
    blocks = deep // BLOCK
    streams = reduce_plan(n_mp, n_dp, width)
    groups = small_groups(n_mp, n_dp)
    total = images * patches
    stage_rows = [have for _, _, stages in streams for _, have, _ in stages]
    n_ids = 1 + len(stage_rows)
    team = groups[0][1] * groups[0][2]
    n_small = 2 + team - 1 + sum(size * across - 1 for _, size, across in groups)
    s_rows = SPACE // team
    hbm, vmem = pl.BlockSpec(memory_space=pl.ANY), pl.BlockSpec(memory_space=pltpu.VMEM)
    dma = pltpu.SemaphoreType.DMA
    scratch = [
        pltpu.VMEM((images, width, patches), BF),
        pltpu.VMEM((patches, width), BF),
        pltpu.VMEM((images, patches, width), BF),
        pltpu.VMEM((total, width), BF),
        pltpu.VMEM((total, width), BF),
        pltpu.VMEM((total // 2, max(deep, 2 * (-(-total // 128) * 128))), BF),
        pltpu.VMEM((2, 2, width, hidden), BF),
        pltpu.VMEM((total // 2, width), F32),
        pltpu.VMEM((patches, width), F32),
        pltpu.VMEM((total, 128), F32),
        pltpu.VMEM((2, 2, total, BLOCK), BF),
        pltpu.VMEM((width, deep), BF),
        pltpu.VMEM((deep, width), BF),
        pltpu.VMEM((2, width, BLOCK), BF),
        pltpu.VMEM((blocks, width, BLOCK), BF),
        [pltpu.VMEM((blocks, rows, BLOCK), BF) for rows in stage_rows],
        pltpu.VMEM((width, SPACE), BF),
        pltpu.VMEM((SPACE, width), BF),
        pltpu.VMEM((width, SPACE), BF),
        pltpu.VMEM((SPACE, hidden), BF),
        pltpu.VMEM((hidden, SPACE), BF),
        pltpu.VMEM((hidden, SPACE), BF),
        pltpu.VMEM((SPACE, hidden), BF),
        pltpu.VMEM((8, width), F32),
        pltpu.VMEM((blocks, 8, BLOCK), F32),
        pltpu.VMEM((2, width, 128), F32),
        pltpu.VMEM((blocks, 8, BLOCK), F32),
        pltpu.VMEM((8, width), F32),
        pltpu.VMEM((width, 128), F32),
        pltpu.VMEM((2 * SPACE, hidden), F32),
        pltpu.VMEM((2 * SPACE, hidden), BF),
        pltpu.VMEM((SPACE, hidden), BF),
        pltpu.VMEM((len(groups), team, s_rows, hidden), BF),
        pltpu.VMEM((s_rows, hidden), BF),
        pltpu.VMEM((SPACE, hidden), BF),
        dma((n_mp - 1, images)),
        dma((n_mp, images)),
        dma((images,)),
        dma((1,)),
        dma((2,)),
        dma((1,)),
        dma((2, 2)),
        dma((2, 2, 2, 2)),
        dma((2, 2)),
        dma((n_mp - 1, images)),
        dma((n_mp, images)),
        dma((images,)),
        dma((n_ids, blocks)),
        dma((n_ids, blocks)),
        dma((n_ids + len(streams), blocks)),
        dma((n_ids + len(streams), blocks)),
        dma((len(streams), blocks)),
        dma((n_small,)),
        dma((n_small,)),
        dma((1,)),
    ]
    out, dtok, gw, smt, _, _ = pl.pallas_call(
        functools.partial(layer_kernel, n_mp, n_dp, streams, groups),
        out_shape=(
            jax.ShapeDtypeStruct(cot.shape, BF),
            jax.ShapeDtypeStruct(tokens.shape, BF),
            jax.ShapeDtypeStruct((2, width, deep), BF),
            jax.ShapeDtypeStruct((2 * SPACE, hidden), BF),
            jax.ShapeDtypeStruct((images, 2, width, hidden), BF),
            jax.ShapeDtypeStruct((2, total, deep), BF),
        ),
        in_specs=[hbm] * 4 + [vmem] * 10,
        out_specs=(hbm,) * 6,
        scratch_shapes=scratch,
        compiler_params=pltpu.CompilerParams(
            collective_id=0, has_side_effects=True, vmem_limit_bytes=VMEM_LIMIT
        ),
    )(tokens, cot, w1, w2, g1, c1, tw1, tb1, tw2, tb2, g2, c2, b1, b2)
    full = lambda n: jax.ShapeDtypeStruct((n,), F32)
    out_spec = pl.BlockSpec((total, width // blocks), lambda j: (0, j))
    dtok_spec = pl.BlockSpec((n_mp * images, local // blocks, patches), lambda j: (0, j, 0))
    results = pl.pallas_call(
        finish_kernel,
        grid=(blocks,),
        out_shape=(
            jax.ShapeDtypeStruct(out.shape, BF),
            jax.ShapeDtypeStruct(dtok.shape, BF),
            full(width),
            full(width),
            jax.ShapeDtypeStruct((patches, hidden), F32),
            full(hidden),
            jax.ShapeDtypeStruct((patches, hidden), F32),
            full(patches),
            full(width),
            full(width),
            jax.ShapeDtypeStruct((width, deep), F32),
            full(deep),
            jax.ShapeDtypeStruct((deep, width), F32),
            full(width),
        ),
        in_specs=[out_spec, dtok_spec, pl.BlockSpec((2, width, BLOCK), lambda j: (0, 0, j)), vmem],
        out_specs=(
            (out_spec, dtok_spec)
            + (vmem,) * 8
            + (
                pl.BlockSpec((width, BLOCK), lambda j: (0, j)),
                vmem,
                pl.BlockSpec((BLOCK, width), lambda j: (j, 0)),
                vmem,
            )
        ),
        compiler_params=pltpu.CompilerParams(vmem_limit_bytes=VMEM_LIMIT),
    )(out, dtok, gw, smt)
    out, dtok, *grads = results
    grads[4] = grads[4].T
    return (out.reshape(patches, images, width).transpose(1, 0, 2), dtok.transpose(0, 2, 1), *grads)


def solution(mesh):
    placed = (P("dp", None, "mp"), P(("dp", "mp"), None, None)) + (P(),) * 12
    return jax.shard_map(body, mesh=mesh, in_specs=placed, out_specs=(placed[1], placed[0]) + (P(),) * 12, check_vma=False)
```
